256 devices in a mesh: seq: 8 (over y, x_hi), dp: 32 (over x_lo, z, core).
Axes of the slice: x: 4 (x_hi: 2, x_lo: 2; x = x_hi * 2 + x_lo), y: 4, z: 8, core: 2. Of those that a mesh axis runs over, the one named last changes fastest.
Arguments:
- queries: bfloat16 [32, 2048, 2048], P('dp', 'seq'), may hold values from -150 to 150
- group_memory: bfloat16 [32, 2048, 2, 896], P('dp', 'seq'), may hold values from -160 to 160
- nb_shard: int32 [32, 32, 2, 128, 1], P('dp', 'seq'), may hold values from 0 to 31; in each aligned block of 1024 rows (0 to 1023, 1024 to 2047, ..., all dimensions but the last counted through in order) at most 48 rows name the same one
- nb_row: int32 [32, 32, 2, 128], P('dp', 'seq'), may hold values from 0 to 2047
- embed: bfloat16 [65536, 896], P('dp'), may hold values from -6 to 6
- w_query_enc: bfloat16 [896, 896], P(None, 'dp'), may hold values from -0.1875 to 0.1875
- w_out_enc: bfloat16 [896, 896], P(None, 'dp'), may hold values from -0.1875 to 0.1875
- w_kv_cca: bfloat16 [896, 4096], P(None, 'dp'), may hold values from -0.1875 to 0.1875
Outputs:
- cca_out: bfloat16 [32, 2048, 2048], P('dp', 'seq')
The draws below stay inside these ranges and needn't reach their ends.
Inputs may be any that keep to these rules, and one draw needn't show every extreme that they name: `nb_shard`: in each aligned block of the 1024 neighbour tokens of one device, no value is named more than 48 times, a bound that some block reaches.
All inputs are finite; a program needn't handle non-finite values.
Results may differ from the reference program's by a relative error of at most 0.02.
The reference program's roundings to bfloat16 on the way count: a program that leaves them out, or rounds other values in their place, can miss the bound.
Values may be sent and summed in bfloat16 or wider, within the bound.
A program may use at most 128 MiB of HBM per device.

```python
import math
import jax
import jax.numpy as jnp
import numpy as np
from jax import lax

CH_DEV = 4
GROUP = 64
NB = 2
NR = 128
ENC = 896
ENC_HD = 64
HQ = 16
HD = 128
VOC_DEV = 2048
BATCH = 32
GROUPS = 32
SEQ_LEN = 2048
VOCAB = 65536
QW = 2048
ENC_HEADS = 14
CAP = 48
N_DP = 32


def draw_queries(key, part):
    key = jax.random.fold_in(key, 5)
    second_key = jax.random.fold_in(key, 1)
    shape = (BATCH, SEQ_LEN, QW)
    values = jnp.clip(jax.random.normal(second_key, shape, jnp.float32), -4.0, 4.0)
    return values.astype(jnp.bfloat16)


def draw_group_memory(key, part):
    key = jax.random.fold_in(key, 11)
    second_key = jax.random.fold_in(key, 1)
    shape = (BATCH, SEQ_LEN, 2, ENC)
    values = jnp.clip(jax.random.normal(second_key, shape, jnp.float32), -4.0, 4.0)
    return values.astype(jnp.bfloat16)


def set_ends(array, stream_key, least, top_value):
    place = [jax.random.randint(jax.random.fold_in(stream_key, axis), (), 0, length) for axis, length in enumerate(array.shape)]
    longest = array.shape.index(max(array.shape))
    beside = place[:longest] + [(place[longest] + 1) % array.shape[longest]] + place[longest + 1:]
    return array.at[tuple(place)].set(least).at[tuple(beside)].set(top_value)


def block_levels(key, dims, pieces, least, top_value):
    def one(position, shards_of):
        draws = jax.random.uniform(jax.random.fold_in(jax.random.fold_in(key, 6), position), (shards_of,), jnp.float32, least / len(pieces), top_value / len(pieces))
        return jnp.repeat(jnp.exp(draws), dims[position] // shards_of).reshape((-1,) + (1,) * (len(dims) - position - 1))

    gain = one(*pieces[0])
    for cut in pieces[1:]:
        gain = gain * one(*cut)
    return gain


def shared_out(own_key, own, number, rows, number_of, top, reach, slope):
    order = jax.random.permutation(own_key, number_of)
    heavy_load, ordinary = load_shares(number_of, rows * top, reach, slope, True), load_shares(number_of, rows * top, reach, slope, False)
    places = jnp.arange(number_of)

    def named(tallies, offset_by):
        used = int((tallies > 0).sum())
        fixed = max(1, used // 4)
        moved = fixed + (places - fixed + offset_by * (used - fixed)) % max(1, number_of - fixed)
        return jnp.zeros((number_of,), jnp.int32).at[order[jnp.where(places < fixed, places, moved)]].set(jnp.asarray(tallies, jnp.int32))

    tallies = jnp.where(number % 4 == 0, named(heavy_load, number // 4), named(ordinary, number - number // 4 - 1))
    mixed = jax.random.permutation(jax.random.fold_in(own, 3), number_of)
    giver, sink = mixed[0:number_of // 2 * 2:2], mixed[1:number_of // 2 * 2:2]
    margin = jnp.minimum(tallies[giver] - 1, reach - tallies[sink]) // 2
    margin = jnp.where((giver == order[0]) | (sink == order[0]) | (tallies[sink] == 0), 0, jnp.maximum(margin, 0))
    moved = jax.random.randint(jax.random.fold_in(own, 4), (number_of // 2,), 0, 1 << 20) % (margin + 1)
    tallies = tallies.at[giver].add(-moved).at[sink].add(moved)
    items = jnp.searchsorted(jnp.cumsum(tallies), jnp.arange(rows * top), side="right").astype(jnp.int32)
    table = items.reshape(top, rows).T
    table = table[jax.random.permutation(jax.random.fold_in(own, 1), rows)]
    offset_by = jax.random.randint(jax.random.fold_in(own, 2), (rows, 1), 0, top)
    return jnp.take_along_axis(table, (jnp.arange(top)[None, :] + offset_by) % top, axis=1)


def load_shares(count, total, bound, skew, full):
    portions = [(1 << 20) // math.isqrt(rank ** skew) + 1 for rank in range(1, count + 1)]
    largest = bound if full else min(bound, max(-(-total // count), total * portions[0] // sum(portions)))
    least = 1 if total - largest >= count - 1 else 0
    holding, spare = [largest] + [least] * (count - 1), total - largest - least * (count - 1)
    while spare > 0:
        movable = [i for i in range(1, count) if holding[i] < largest] or [i for i in range(1, count) if holding[i] < bound]
        mass, left = sum([portions[i] for i in movable]), spare
        for i in movable:
            more = min(bound - holding[i], max(1, left * portions[i] // mass), spare)
            holding[i] = holding[i] + more
            spare = spare - more
    return np.array(holding)


def bell_draw(rng, shape, deviation, most, cuts=(), kind=jnp.bfloat16):
    array = jax.random.normal(rng, shape, jnp.float32) * deviation
    if len(cuts) > 0:
        array = block_levels(rng, shape, cuts, -0.22, 0.18) * array
    return jnp.clip(array, min=-most, max=most).astype(kind)


def setup_inputs(seed: int = 0) -> dict:
    key_list = jax.random.split(jax.random.key(seed), 9)
    queries = draw_queries(jax.random.fold_in(key_list[8], 71), 0)
    group_memory = draw_group_memory(jax.random.fold_in(key_list[8], 71), 0)
    nb_shard_keys = jax.random.split(jax.random.fold_in(key_list[2], 1), BATCH * GROUPS * NB * NR // (CH_DEV * NB * NR))
    nb_shard_turns = jax.random.permutation(jax.random.fold_in(key_list[2], 3), BATCH * GROUPS * NB * NR // (CH_DEV * NB * NR))
    nb_shard = jax.vmap(lambda own, number: shared_out(jax.random.fold_in(key_list[2], 2), own, number, CH_DEV * NB * NR, N_DP, 1, CAP, 1))(nb_shard_keys, nb_shard_turns).reshape((BATCH, GROUPS, NB, NR, 1))
    nb_row = set_ends(jax.random.randint(key_list[3], (BATCH, GROUPS, NB, NR), 0, VOC_DEV), jax.random.fold_in(key_list[3], 1), 0, VOC_DEV - 1).astype(jnp.int32)
    embed = bell_draw(key_list[4], (VOCAB, ENC), 1.0, 6.0, ((0, 32),))
    w_query_enc = bell_draw(key_list[5], (ENC, ENC), ENC ** -0.5, 0.1875, ((1, 32),))
    w_out_enc = bell_draw(key_list[6], (ENC, ENC), ENC ** -0.5, 0.1875, ((1, 32),))
    w_kv_cca = bell_draw(key_list[7], (ENC, 2 * QW), ENC ** -0.5, 0.1875, ((1, 32),))
    return dict(queries=queries, group_memory=group_memory, nb_shard=nb_shard, nb_row=nb_row, embed=embed, w_query_enc=w_query_enc, w_out_enc=w_out_enc, w_kv_cca=w_kv_cca)


def soft_rounded(scores):
    rounded = lax.optimization_barrier(jax.nn.softmax(scores, axis=-1).astype(jnp.bfloat16))
    return rounded.astype(jnp.float32)

def one_sequence(queries_seq, memory, shard_ids, row_ids, embed, w_query_enc, w_out_enc, w_kv_cca):
    group_count = SEQ_LEN // GROUP
    span = NB * NR
    token_ids = (shard_ids[..., 0] * VOC_DEV + row_ids).reshape(-1).astype(jnp.int32)
    neighbour_rows = jnp.take(embed, token_ids, axis=0)
    wide_rows = neighbour_rows.astype(jnp.float32)
    normed = (wide_rows * lax.rsqrt(lax.optimization_barrier(jnp.mean(wide_rows * wide_rows, axis=-1, keepdims=True)) + 1e-06)).astype(jnp.bfloat16)
    enc_query = jnp.dot(normed, w_query_enc, preferred_element_type=jnp.float32).astype(jnp.bfloat16)
    head_query = enc_query.reshape(group_count, span, ENC_HEADS, ENC_HD).astype(jnp.float32)
    group_mem = memory.reshape(group_count, GROUP, 2, ENC_HEADS, ENC_HD).astype(jnp.float32)
    scores = jnp.einsum('cnhd,cmhd->chnm', head_query, group_mem[:, :, 0]) * (1.0 / math.sqrt(ENC_HD))
    mixed_heads = jnp.einsum('chnm,cmhd->cnhd', soft_rounded(scores), group_mem[:, :, 1]).astype(jnp.bfloat16)
    mixed_heads = mixed_heads.reshape(group_count * span, ENC)
    projected = jnp.dot(mixed_heads, w_out_enc, preferred_element_type=jnp.float32)
    encoded = (wide_rows + projected).astype(jnp.bfloat16)
    keys_values = jnp.dot(encoded, w_kv_cca, preferred_element_type=jnp.float32).astype(jnp.bfloat16)
    keys_values = keys_values.reshape(group_count, span, 2 * QW)
    stacked = jnp.concatenate([jnp.zeros((1, span, 2 * QW), jnp.bfloat16), keys_values], axis=0)
    padded = jnp.concatenate([jnp.zeros((1, QW), jnp.bfloat16), queries_seq, jnp.zeros((GROUP - 1, QW), jnp.bfloat16)], axis=0)
    padded = padded.reshape(group_count + 1, GROUP, HQ, HD).astype(jnp.float32)
    cca_keys = stacked[:, :, :QW].reshape(group_count + 1, span, HQ, HD).astype(jnp.float32)
    cca_values = stacked[:, :, QW:].reshape(group_count + 1, span, HQ, HD).astype(jnp.float32)
    cca_scores = jnp.einsum('bqhd,bkhd->bhqk', padded, cca_keys) * (1.0 / math.sqrt(HD))
    attended = jnp.einsum('bhqk,bkhd->bqhd', soft_rounded(cca_scores), cca_values).astype(jnp.bfloat16)
    return attended.reshape((group_count + 1) * GROUP, QW)[1:SEQ_LEN + 1]

def reference(queries, group_memory, nb_shard, nb_row, embed, w_query_enc, w_out_enc, w_kv_cca):

    def per_sequence(bundle):
        return one_sequence(bundle[0], bundle[1], bundle[2], bundle[3], embed, w_query_enc, w_out_enc, w_kv_cca)
    return lax.map(per_sequence, (queries, group_memory, nb_shard, nb_row))
```

```python
import functools
import math

import jax
import jax.numpy as jnp
from jax import lax
from jax.experimental import pallas as pl
from jax.experimental.pallas import tpu as pltpu
from jax.sharding import PartitionSpec as P

MESH = pl.DeviceIdType.MESH
BF = jnp.bfloat16
F32 = jnp.float32
ENC = 896
QW = 2048
HQ = 16
HD = 128
CAP = 48
TOK = 1024
PAIRS = 7
UNITS = 4
UROWS = 384
SLOTS = 1536
NEG = -1e30


def nt(a, b):
    return lax.dot_general(a, b, (((1,), (1,)), ((), ())), preferred_element_type=F32)


def nn(a, b):
    return jnp.dot(a, b, preferred_element_type=F32)


def iota(shape, dim):
    return lax.broadcasted_iota(jnp.int32, shape, dim)


def offset_of(k):
    base = 4 - (k + 1) // 2
    odd = lax.rem(k, 2)
    return lax.rem(odd * base + (1 - odd) * (8 - base), 8)


def body(
    own_ref, rid_ref, emb_hbm, wq_ref, wo_ref, wkv_ref, gm_hbm, q_hbm,
    out_ref,
    emb, gm, q, packk, packq, gk, gq, send, rows, onehot, keys, valt, wqt, wot, pieces,
    kbd, vbd, reqs, rreqs, icol, gcol, gpos, xenc, qenc, mixed, qnext, fin, outp,
    lsem, zks, zkr, zqs, zqr, yks, ykr, yqs, yqr, xks, xkr, xqs, xqr, sks, skr, sqs, sqr,
    rs, rr, ts, tr, ns, nr, fs, fr,
):
    seq = lax.axis_index("seq")
    dp = lax.axis_index("dp")
    xl = dp // 16
    z = lax.rem(dp // 2, 8)
    c = lax.rem(dp, 2)
    y = seq // 2
    xh = lax.rem(seq, 2)
    x = xh * 2 + xl
    xo = 1 - xl

    def at_x(xx):
        return (y * 2 + xx // 2, lax.rem(xx, 2) * 16 + z * 2 + c)

    partner = at_x(x + 1 - 2 * xl)
    wrap = at_x(lax.rem(x + 3 + 2 * xl, 4))
    sib = (seq, xl * 16 + z * 2 + 1 - c)
    nxt = (lax.rem(seq + 1, 8), dp)
    prv = (lax.rem(seq + 7, 8), dp)

    c_emb = pltpu.make_async_copy(emb_hbm, emb, lsem.at[0])
    c_q = pltpu.make_async_copy(q_hbm, q, lsem.at[1])
    c_gm = pltpu.make_async_copy(gm_hbm, gm, lsem.at[2])
    c_emb.start()
    c_q.start()
    c_gm.start()

    bar = pltpu.get_barrier_semaphore()

    def greet(k, _):
        pl.semaphore_signal(bar, inc=1, device_id=(seq, lax.rem(dp + k, 32)), device_id_type=MESH)
        return 0

    lax.fori_loop(1, 32, greet, 0)
    for k in range(1, 4):
        pl.semaphore_signal(bar, inc=1, device_id=(lax.rem(y + k, 4) * 2 + xh, dp), device_id_type=MESH)
    for dev in (partner, wrap, nxt, prv):
        pl.semaphore_signal(bar, inc=1, device_id=dev, device_id_type=MESH)

    kvt = wkv_ref[...].T
    packk[...] = kvt.reshape(4, 32, ENC)
    zero4 = jnp.zeros((4, ENC), BF)
    packq[0] = wq_ref[0:16, :]
    packq[1] = jnp.concatenate([wq_ref[16:28, :].astype(F32), zero4.astype(F32)], axis=0).astype(BF)
    packq[2] = wo_ref[0:16, :]
    packq[3] = jnp.concatenate([wo_ref[16:28, :].astype(F32), zero4.astype(F32)], axis=0).astype(BF)

    pl.semaphore_wait(bar, 38)

    def rdma(src, dst, s, r, dev):
        return pltpu.make_async_remote_copy(
            src_ref=src, dst_ref=dst, send_sem=s, recv_sem=r, device_id=dev, device_id_type=MESH
        )

    KQ = (packq, gq, zqs, zqr, yqs, yqr, xqs, xqr, sqs, sqr)
    KK = (packk, gk, zks, zkr, yks, ykr, xks, xkr, sks, skr)

    def zcopy(kind, zz):
        pack, g, s, r = kind[0], kind[1], kind[2], kind[3]
        return rdma(pack.at[y], g.at[xl, c, z, y], s.at[zz], r.at[z], (seq, xl * 16 + zz * 2 + c))

    def zcopy_in(kind, zz):
        pack, g, s, r = kind[0], kind[1], kind[2], kind[3]
        return rdma(pack.at[y], g.at[xl, c, zz, y], s.at[zz], r.at[zz], (seq, xl * 16 + zz * 2 + c))

    def ycopy(kind, zz, yy):
        g, s, r = kind[1], kind[4], kind[5]
        p = g.at[xl, c, zz, y]
        return rdma(p, p, s.at[zz, yy], r.at[zz, y], (yy * 2 + xh, dp))

    def ycopy_in(kind, zz, yy):
        g, s, r = kind[1], kind[4], kind[5]
        p = g.at[xl, c, zz, yy]
        return rdma(p, p, s.at[zz, yy], r.at[zz, yy], (yy * 2 + xh, dp))

    def xcopy(kind, zz, dev):
        g, s, r = kind[1], kind[6], kind[7]
        p = g.at[xl, c, zz]
        return rdma(p, p, s.at[zz], r.at[zz], dev)

    def xcopy_in(kind, zz):
        g, s, r = kind[1], kind[6], kind[7]
        p = g.at[xo, c, zz]
        return rdma(p, p, s.at[zz], r.at[zz], partner)

    def scopy(kind, a, zz):
        g, s, r = kind[1], kind[8], kind[9]
        p = g.at[a, c, zz]
        return rdma(p, p, s.at[a, zz], r.at[a, zz], sib)

    def scopy_in(kind, a, zz):
        g, s, r = kind[1], kind[8], kind[9]
        p = g.at[a, 1 - c, zz]
        return rdma(p, p, s.at[a, zz], r.at[a, zz], sib)

    def loop(lo, hi, fn):
        def step(k, _):
            fn(k)
            return 0

        lax.fori_loop(lo, hi, step, 0)

    def z_send(kind):
        loop(1, 8, lambda k: zcopy(kind, lax.rem(z + k, 8)).start())

    def y_send(kind, lo, hi):
        def one(k):
            zz = lax.rem(z + k, 8)
            zcopy_in(kind, zz).wait_recv()
            for j in range(1, 4):
                ycopy(kind, zz, lax.rem(y + j, 4)).start()

        loop(lo, hi, one)

    def x_send(kind, lo, hi):
        def one(k):
            zz = lax.rem(z + k, 8)

            @pl.when(k > 0)
            def _():
                for j in range(1, 4):
                    ycopy_in(kind, zz, lax.rem(y + j, 4)).wait_recv()

            @pl.when(lax.rem(zz, 4) == 0)
            def _():
                xcopy(kind, zz, partner).start()

            @pl.when(lax.rem(zz, 4) != 0)
            def _():
                xcopy(kind, zz, wrap).start()

            scopy(kind, xl, zz).start()

        loop(lo, hi, one)

    def x_pass(kind, lo, hi):
        def one(k):
            zz = lax.rem(z + k, 8)
            xcopy_in(kind, zz).wait_recv()
            scopy(kind, xo, zz).start()

        loop(lo, hi, one)

    def s_wait(kind):
        def one(zz):
            for a in range(2):
                scopy_in(kind, a, zz).wait_recv()

        loop(0, 8, one)

    def drain(kind):
        def one(zz):
            xcopy(kind, zz, partner).wait_send()
            for a in range(2):
                scopy(kind, a, zz).wait_send()

        loop(0, 8, one)

        def two(k):
            zz = lax.rem(z + k, 8)
            zcopy(kind, zz).wait_send()
            for j in range(1, 4):
                ycopy(kind, zz, lax.rem(y + j, 4)).wait_send()

        loop(1, 8, two)

    z_send(KQ)
    z_send(KK)
    c_lq = pltpu.make_async_copy(packq, gq.at[xl, c, z], lsem.at[3])
    c_lk = pltpu.make_async_copy(packk, gk.at[xl, c, z], lsem.at[4])
    c_lq.start()
    c_lk.start()

    own = own_ref[...]
    marks = (iota((32, TOK), 0) == own).astype(F32)
    upper = (iota((128, 128), 0) <= iota((128, 128), 1)).astype(BF)
    total = jnp.zeros((32, 1), F32)
    parts = []
    for k in range(TOK // 128):
        m = marks[:, k * 128 : (k + 1) * 128]
        cum = nn(m.astype(BF), upper) + total
        total = cum[:, 127:128]
        parts.append(jnp.sum(m * (cum - 1.0), axis=0, keepdims=True))
    slot = jnp.concatenate(parts, axis=1).astype(jnp.int32)
    place = (iota((128, TOK), 0) == slot).astype(BF)
    rid = rid_ref[...]
    high = (rid // 64).astype(F32)
    low = (rid - (rid // 64) * 64).astype(F32)
    group = (iota((1, TOK), 1) // 256 + 1).astype(F32)
    hi = nt((marks * high).astype(BF), place)
    lo = nt((marks * low).astype(BF), place)
    asked = (hi * 64.0 + lo).astype(jnp.int32)
    for d in range(32):
        reqs[d] = asked[d : d + 1, :]

    def tcopy(d):
        return rdma(reqs.at[d], rreqs.at[dp], ts.at[d], tr.at[dp], (seq, d))

    def tcopy_in(d):
        return rdma(reqs.at[d], rreqs.at[d], ts.at[d], tr.at[d], (seq, d))

    loop(1, 32, lambda k: tcopy(lax.rem(dp + k, 32)).start())
    c_lt = pltpu.make_async_copy(reqs.at[dp], rreqs.at[dp], lsem.at[5])
    c_lt.start()
    c_q.wait()
    n_out = rdma(q.at[pl.ds(0, 64)], qnext, ns, nr, prv)
    n_out.start()

    groups = nt(place, (marks * group).astype(BF))
    for d in range(32):
        place_d = ((d // 2) % 8) * 4 + (d // 16) * 2 + d % 2
        gcol[place_d // 4, (place_d % 4) * CAP : (place_d % 4 + 1) * CAP, :] = jnp.broadcast_to(
            groups[0:CAP, d : d + 1], (CAP, 128)
        )

    c_gm.wait()
    lane_low = iota((256, 128), 1) < 64
    for p in range(PAIRS):
        for src, dst in ((0, kbd), (1, vbd)):
            m = gm[src, :, p * 128 : (p + 1) * 128].astype(F32)
            dst[p, 0:256, :] = jnp.where(lane_low, m, 0.0).astype(BF)
            dst[p, 256:512, :] = jnp.where(lane_low, 0.0, m).astype(BF)

    y_send(KQ, 1, 8)

    c_lt.wait()
    loop(1, 32, lambda k: tcopy_in(lax.rem(dp + k, 32)).wait_recv())
    got = jnp.concatenate([rreqs[d] for d in range(32)], axis=0).astype(F32).T
    for d in range(32):
        icol[d] = jnp.broadcast_to(got[0:CAP, d : d + 1], (CAP, 128)).astype(jnp.int32)
    c_emb.wait()

    def dest(zz, j):
        return (j // 2) * 16 + zz * 2 + j % 2

    def rcopy(d, zz, j):
        return rdma(send.at[zz, j], rows.at[z, xl * 2 + c], rs.at[d], rr.at[dp], (seq, d))

    def rcopy_in(d, zz, j):
        return rdma(send.at[zz, j], rows.at[zz, j], rs.at[d], rr.at[d], (seq, d))

    def gather(u):
        for half in range(2):
            zz = lax.rem(z + offset_of(2 * u + half), 8)
            for j in range(4):
                idx = icol[dest(zz, j)]
                base = half * 192 + j * CAP
                for k in range(16):
                    onehot[base : base + CAP, k * 128 : (k + 1) * 128] = (
                        (iota((CAP, 128), 1) + k * 128) == idx
                    ).astype(BF)
        for n in range(7):
            got_rows = nn(onehot[...], emb[:, n * 128 : (n + 1) * 128]).astype(BF)
            for half in range(2):
                zz = lax.rem(z + offset_of(2 * u + half), 8)
                for j in range(4):
                    base = half * 192 + j * CAP
                    send[zz, j, :, n * 128 : (n + 1) * 128] = got_rows[base : base + CAP]
        for half in range(2):
            zz = lax.rem(z + offset_of(2 * u + half), 8)
            for j in range(4):
                d = dest(zz, j)

                @pl.when(d != dp)
                def _():
                    rcopy(d, zz, j).start()

                @pl.when(d == dp)
                def _():
                    pltpu.make_async_copy(send.at[zz, j], rows.at[zz, j], lsem.at[6]).start()

    loop(0, 2, gather)
    y_send(KK, 1, 4)
    loop(2, 4, gather)
    c_lq.wait()
    c_lk.wait()
    x_send(KQ, 0, 8)
    y_send(KK, 4, 8)
    x_send(KK, 0, 4)
    x_pass(KQ, 0, 8)
    s_wait(KQ)

    f = iota((448, 512), 0)
    perm = (iota((448, 512), 1) == f + 4 * lax.shift_right_logical(f * 2341, 16)).astype(BF)
    for which, dst in ((0, wqt), (2, wot)):
        for a in range(2):
            for d in range(16):
                pieces[d * 32 : (d + 1) * 32, :] = gq[a, d % 2, d // 2, which : which + 2].reshape(32, ENC)
            dst[a * 448 : (a + 1) * 448, :] = nn(perm, pieces[...]).astype(BF)

    memory_group = (lax.rem(iota((1, 512), 1), 256) // 64 + 1).astype(F32)

    def encode(u):
        for half in range(2):
            zz = lax.rem(z + offset_of(2 * u + half), 8)
            for j in range(4):
                d = dest(zz, j)

                @pl.when(d != dp)
                def _():
                    rcopy_in(d, zz, j).wait_recv()

                @pl.when(d == dp)
                def _():
                    pltpu.make_async_copy(send.at[zz, j], rows.at[zz, j], lsem.at[6]).wait()

        zs = [lax.rem(z + offset_of(2 * u + half), 8) for half in range(2)]
        wide = jnp.concatenate([rows[zz].reshape(192, ENC) for zz in zs], axis=0).astype(F32)
        gp = jnp.concatenate([gcol[zz] for zz in zs], axis=0)
        at = pl.multiple_of(u * UROWS, UROWS)
        gpos[pl.ds(at, UROWS), :] = gp
        inv = lax.rsqrt(jnp.mean(wide * wide, axis=-1, keepdims=True) + 1e-6)
        normed = (wide * inv).astype(BF)
        qenc[...] = nt(normed, wqt[...]).astype(BF)
        allowed = jnp.concatenate([gp] * 4, axis=1) == memory_group

        def pair(p):
            lanes = pl.ds(pl.multiple_of(p * 128, 128), 128)
            s = nt(qenc[:, lanes], kbd[p]) * 0.125
            s = jnp.where(allowed, s, NEG)
            ws = []
            for half in range(2):
                sh = s[:, half * 256 : (half + 1) * 256]
                e = jnp.exp(sh - jnp.max(sh, axis=-1, keepdims=True))
                ws.append((e * (1.0 / jnp.sum(e, axis=-1, keepdims=True))).astype(BF))
            w = jnp.concatenate(ws, axis=1)
            mixed[:, lanes] = nn(w, vbd[p]).astype(BF)

        loop(0, PAIRS, pair)
        xenc[u] = (wide + nt(mixed[...], wot[...])).astype(BF)

    def project(u):
        at = pl.multiple_of(u * UROWS, UROWS)

        def head(h):
            wk = gk[0, lax.rem(h, 2), h // 2].reshape(128, ENC)
            keys[h, pl.ds(at, UROWS), :] = nt(xenc[u], wk).astype(BF)
            wv = gk[1, lax.rem(h, 2), h // 2].reshape(128, ENC)
            valt[h, :, pl.ds(at, UROWS)] = nt(wv, xenc[u]).astype(BF)

        loop(0, HQ, head)

    encode(0)
    x_send(KK, 4, 8)
    encode(1)
    x_pass(KK, 0, 8)
    s_wait(KK)
    project(0)
    project(1)

    def last(u):
        encode(u)
        project(u)

    loop(2, 4, last)

    n_out.wait()
    first = iota((64, QW), 0) < 63
    mine = q[0:64, :]
    q[0:64, :] = jnp.where(first, qnext[...].astype(F32), mine.astype(F32)).astype(BF)
    r1 = iota((1, 256), 1) + 1
    qgroup = jnp.where(r1 < 64, 4, r1 // 64).astype(F32)
    scale = 1.0 / math.sqrt(HD)

    def attend(h):
        lanes = pl.ds(pl.multiple_of(h * HD, HD), HD)
        s = nt(keys[h], q[:, lanes]) * scale
        gp = gpos[...]
        s = jnp.where(jnp.concatenate([gp, gp], axis=1) == qgroup, s, NEG)
        e = jnp.exp(s - jnp.max(s, axis=0, keepdims=True))
        w = (e * (1.0 / jnp.sum(e, axis=0, keepdims=True))).astype(BF)
        outp[:, lanes] = nn(valt[h], w).T.astype(BF)

    def fcopy(k):
        p = pl.ds(k * 512, 512)
        return rdma(outp.at[pl.ds(0, 64), p], fin.at[:, p], fs.at[k], fr.at[k], nxt)

    for k in range(4):
        loop(4 * k, 4 * k + 4, attend)
        fcopy(k).start()

    drain(KQ)
    drain(KK)
    loop(1, 32, lambda k: tcopy(lax.rem(dp + k, 32)).wait_send())

    def rdone(i):
        zz = i // 4
        j = lax.rem(i, 4)
        d = (j // 2) * 16 + zz * 2 + lax.rem(j, 2)

        @pl.when(d != dp)
        def _():
            rcopy(d, zz, j).wait_send()

    loop(0, 32, rdone)

    out_ref[64:256, :] = outp[64:256, :]
    for k in range(4):
        fcopy(k).wait()
    keep = (iota((64, QW), 0) < 63).astype(F32)
    some = jnp.where(seq > 0, 1.0, 0.0).astype(F32)
    mine = outp[0:64, :].astype(F32)
    came = fin[...].astype(F32)
    out_ref[0:64, :] = jnp.where(keep > 0.5, came * some, mine).astype(BF)


def shards(queries, group_memory, nb_shard, nb_row, embed, w_query_enc, w_out_enc, w_kv_cca):
    own = nb_shard.reshape(1, TOK)
    rid = nb_row.reshape(1, TOK)
    gm = group_memory[0].transpose(1, 0, 2)
    D = pltpu.SemaphoreType.DMA
    vm = lambda *s: pltpu.VMEM(s, BF)
    any_ = pl.BlockSpec(memory_space=pl.ANY)
    here = pl.BlockSpec(memory_space=pltpu.VMEM)
    out = pl.pallas_call(
        body,
        out_shape=jax.ShapeDtypeStruct((256, QW), BF),
        in_specs=[here, here, any_, here, here, here, any_, any_],
        out_specs=here,
        scratch_shapes=[
            vm(2048, ENC), vm(2, 256, ENC), vm(256, QW), vm(4, 32, ENC), vm(4, 16, ENC),
            vm(2, 2, 8, 4, 32, ENC), vm(2, 2, 8, 4, 16, ENC),
            vm(8, 4, CAP, ENC), vm(8, 4, CAP, ENC), vm(UROWS, 2048),
            vm(HQ, SLOTS, HD), vm(HQ, HD, SLOTS), vm(ENC, ENC), vm(ENC, ENC), vm(512, ENC),
            vm(PAIRS, 512, 128), vm(PAIRS, 512, 128),
            pltpu.VMEM((32, 1, 128), jnp.int32), pltpu.VMEM((32, 1, 128), jnp.int32),
            pltpu.VMEM((32, CAP, 128), jnp.int32),
            pltpu.VMEM((8, 192, 128), F32), pltpu.VMEM((SLOTS, 128), F32),
            vm(UNITS, UROWS, ENC), vm(UROWS, ENC), vm(UROWS, ENC),
            vm(64, QW), vm(64, QW), vm(256, QW),
            D((7,)), D((8,)), D((8,)), D((8,)), D((8,)),
            D((8, 4)), D((8, 4)), D((8, 4)), D((8, 4)),
            D((8,)), D((8,)), D((8,)), D((8,)),
            D((2, 8)), D((2, 8)), D((2, 8)), D((2, 8)),
            D((32,)), D((32,)), D((32,)), D((32,)),
            D(()), D(()), D((4,)), D((4,)),
        ],
        compiler_params=pltpu.CompilerParams(
            collective_id=1, has_side_effects=True, vmem_limit_bytes=62 << 20
        ),
    )(own, rid, embed, w_query_enc.T, w_out_enc.T, w_kv_cca, gm, queries[0])
    return out[None]


def solution(mesh):
    in_specs = (
        P("dp", "seq", None),
        P("dp", "seq", None, None),
        P("dp", "seq", None, None, None),
        P("dp", "seq", None, None),
        P("dp", None),
        P(None, "dp"),
        P(None, "dp"),
        P(None, "dp"),
    )
    out_specs = P("dp", "seq", None)
    return jax.shard_map(shards, mesh=mesh, in_specs=in_specs, out_specs=out_specs, check_vma=False)
```

```python
import functools
import math

import jax
import jax.numpy as jnp
from jax import lax
from jax.experimental import pallas as pl
from jax.experimental.pallas import tpu as pltpu
from jax.sharding import PartitionSpec as P

MESH = pl.DeviceIdType.MESH
BF = jnp.bfloat16
F32 = jnp.float32
ENC = 896
QW = 2048
HQ = 16
HD = 128
CAP = 48
TOK = 1024
PAIRS = 7
UNITS = 4
UROWS = 384
NEG = -1e30
LOG2E = math.log2(math.e)


def nt(a, b):
    return lax.dot_general(a, b, (((1,), (1,)), ((), ())), preferred_element_type=F32)


def nn(a, b):
    return jnp.dot(a, b, preferred_element_type=F32)


def iota(shape, dim):
    return lax.broadcasted_iota(jnp.int32, shape, dim)


def offset_of(k):
    base = 4 - (k + 1) // 2
    odd = lax.rem(k, 2)
    return lax.rem(odd * base + (1 - odd) * (8 - base), 8)


def body(
    own_ref, rid_ref, emb_hbm, wq_ref, wo_ref, wkv_ref, gm_hbm, q_hbm,
    out_ref,
    emb, gm, q, packk, packq, gk, gq, send, rows, onehot, keys, vals, wqt, wot, pieces,
    kbd, vbdt, reqs, rreqs, icol, gcol, spos, xtok, qenc, mixed, qnext, qs, fin,
    lsem, zks, zkr, zqs, zqr, yks, ykr, yqs, yqr, xks, xkr, xqs, xqr, sks, skr, sqs, sqr,
    rs, rr, ts, tr, ns, nr, fs, fr,
):
    seq = lax.axis_index("seq")
    dp = lax.axis_index("dp")
    xl = dp // 16
    z = lax.rem(dp // 2, 8)
    c = lax.rem(dp, 2)
    y = seq // 2
    xh = lax.rem(seq, 2)
    x = xh * 2 + xl
    xo = 1 - xl

    def at_x(xx):
        return (y * 2 + xx // 2, lax.rem(xx, 2) * 16 + z * 2 + c)

    partner = at_x(x + 1 - 2 * xl)
    wrap = at_x(lax.rem(x + 3 + 2 * xl, 4))
    sib = (seq, xl * 16 + z * 2 + 1 - c)
    nxt = (lax.rem(seq + 1, 8), dp)
    prv = (lax.rem(seq + 7, 8), dp)

    c_emb = pltpu.make_async_copy(emb_hbm, emb, lsem.at[0])
    c_q = pltpu.make_async_copy(q_hbm, q, lsem.at[1])
    c_gm = pltpu.make_async_copy(gm_hbm, gm, lsem.at[2])
    c_emb.start()
    c_q.start()
    c_gm.start()

    bar = pltpu.get_barrier_semaphore()

    def greet(k, _):
        pl.semaphore_signal(bar, inc=1, device_id=(seq, lax.rem(dp + k, 32)), device_id_type=MESH)
        return 0

    lax.fori_loop(1, 32, greet, 0)
    for k in range(1, 4):
        pl.semaphore_signal(bar, inc=1, device_id=(lax.rem(y + k, 4) * 2 + xh, dp), device_id_type=MESH)
    for dev in (partner, wrap, nxt, prv):
        pl.semaphore_signal(bar, inc=1, device_id=dev, device_id_type=MESH)

    kvt = wkv_ref[...].T
    packk[...] = kvt.reshape(4, 32, ENC)
    zero4 = jnp.zeros((4, ENC), BF)
    packq[0] = wq_ref[0:16, :]
    packq[1] = jnp.concatenate([wq_ref[16:28, :].astype(F32), zero4.astype(F32)], axis=0).astype(BF)
    packq[2] = wo_ref[0:16, :]
    packq[3] = jnp.concatenate([wo_ref[16:28, :].astype(F32), zero4.astype(F32)], axis=0).astype(BF)

    def rdma(src, dst, s, r, dev):
        return pltpu.make_async_remote_copy(
            src_ref=src, dst_ref=dst, send_sem=s, recv_sem=r, device_id=dev, device_id_type=MESH
        )

    KQ = (packq, gq, zqs, zqr, yqs, yqr, xqs, xqr, sqs, sqr)
    KK = (packk, gk, zks, zkr, yks, ykr, xks, xkr, sks, skr)

    def zcopy(kind, way, step):
        pack, g, s, r = kind[0], kind[1], kind[2], kind[3]
        of = lax.rem(z - way * step + 8, 8)
        to = lax.rem(z + way + 8, 8)
        src = pack.at[y] if step == 0 else g.at[xl, c, of, y]
        mark = step if way == 1 else 4 + step
        return rdma(src, g.at[xl, c, of, y], s.at[mark], r.at[of], (seq, xl * 16 + to * 2 + c))

    def zcopy_in(kind, way, step):
        pack, g, s, r = kind[0], kind[1], kind[2], kind[3]
        of = lax.rem(z - way * (step + 1) + 8, 8)
        frm = lax.rem(z + way + 8, 8)
        p = g.at[xl, c, of, y]
        return rdma(p, p, s.at[of], r.at[of], (seq, xl * 16 + frm * 2 + c))

    ZSTEPS = ((0, KQ, 1, 4), (1, KQ, -1, 3), (2, KK, -1, 4), (3, KK, 1, 3))

    def z_step(step):
        for n, kind, way, count in ZSTEPS:
            if 0 < step <= count:
                zcopy_in(kind, way, step - 1).wait_recv()
            if step < count:
                zcopy(kind, way, step).start()

    def ycopy(kind, zz, yy):
        g, s, r = kind[1], kind[4], kind[5]
        p = g.at[xl, c, zz, y]
        return rdma(p, p, s.at[zz, yy], r.at[zz, y], (yy * 2 + xh, dp))

    def ycopy_in(kind, zz, yy):
        g, s, r = kind[1], kind[4], kind[5]
        p = g.at[xl, c, zz, yy]
        return rdma(p, p, s.at[zz, yy], r.at[zz, yy], (yy * 2 + xh, dp))

    def xcopy(kind, zz, dev):
        g, s, r = kind[1], kind[6], kind[7]
        p = g.at[xl, c, zz]
        return rdma(p, p, s.at[zz], r.at[zz], dev)

    def xcopy_in(kind, zz):
        g, s, r = kind[1], kind[6], kind[7]
        p = g.at[xo, c, zz]
        return rdma(p, p, s.at[zz], r.at[zz], partner)

    def scopy(kind, a, zz):
        g, s, r = kind[1], kind[8], kind[9]
        p = g.at[a, c, zz]
        return rdma(p, p, s.at[a, zz], r.at[a, zz], sib)

    def scopy_in(kind, a, zz):
        g, s, r = kind[1], kind[8], kind[9]
        p = g.at[a, 1 - c, zz]
        return rdma(p, p, s.at[a, zz], r.at[a, zz], sib)

    def loop(lo, hi, fn):
        def step(k, _):
            fn(k)
            return 0

        lax.fori_loop(lo, hi, step, 0)

    def y_send(kind):
        def one(k):
            zz = lax.rem(z + k, 8)
            for j in range(1, 4):
                ycopy(kind, zz, lax.rem(y + j, 4)).start()

        loop(1, 8, one)

    def x_send(kind, lo, hi):
        def one(k):
            zz = lax.rem(z + k, 8)

            @pl.when(k > 0)
            def _():
                for j in range(1, 4):
                    ycopy_in(kind, zz, lax.rem(y + j, 4)).wait_recv()

            @pl.when(lax.rem(zz, 4) == 0)
            def _():
                xcopy(kind, zz, partner).start()

            @pl.when(lax.rem(zz, 4) != 0)
            def _():
                xcopy(kind, zz, wrap).start()

            scopy(kind, xl, zz).start()

        loop(lo, hi, one)

    def x_pass(kind, lo, hi):
        def one(k):
            zz = lax.rem(z + k, 8)
            xcopy_in(kind, zz).wait_recv()
            scopy(kind, xo, zz).start()

        loop(lo, hi, one)

    def s_wait(kind):
        def one(zz):
            for a in range(2):
                scopy_in(kind, a, zz).wait_recv()

        loop(0, 8, one)

    def drain(kind):
        def one(zz):
            xcopy(kind, zz, partner).wait_send()
            for a in range(2):
                scopy(kind, a, zz).wait_send()

        loop(0, 8, one)

        def two(k):
            zz = lax.rem(z + k, 8)
            for j in range(1, 4):
                ycopy(kind, zz, lax.rem(y + j, 4)).wait_send()

        loop(1, 8, two)

    own = own_ref[...]
    marks = (iota((32, TOK), 0) == own).astype(F32)
    upper = (iota((128, 128), 0) <= iota((128, 128), 1)).astype(BF)
    total = jnp.zeros((32, 1), F32)
    parts = []
    for k in range(TOK // 128):
        m = marks[:, k * 128 : (k + 1) * 128]
        cum = nn(m.astype(BF), upper) + total
        total = cum[:, 127:128]
        parts.append(jnp.sum(m * (cum - 1.0), axis=0, keepdims=True))
    slot = jnp.concatenate(parts, axis=1).astype(jnp.int32)
    place = (iota((128, TOK), 0) == slot).astype(BF)
    rid = rid_ref[...]
    high = (rid // 64).astype(F32)
    low = (rid - (rid // 64) * 64).astype(F32)
    group = (iota((1, TOK), 1) // 256 + 1).astype(F32)
    hi = nt((marks * high).astype(BF), place)
    lo = nt((marks * low).astype(BF), place)
    asked = (hi * 64.0 + lo).astype(jnp.int32)
    for d in range(32):
        reqs[d] = asked[d : d + 1, :]

    def tcopy(d):
        return rdma(reqs.at[d], rreqs.at[dp], ts.at[d], tr.at[dp], (seq, d))

    def tcopy_in(d):
        return rdma(reqs.at[d], rreqs.at[d], ts.at[d], tr.at[d], (seq, d))

    groups = nt(place, (marks * group).astype(BF))
    for d in range(32):
        place_d = ((d // 2) % 8) * 4 + (d // 16) * 2 + d % 2
        gcol[place_d // 4, (place_d % 4) * CAP : (place_d % 4 + 1) * CAP, :] = jnp.broadcast_to(
            groups[0:CAP, d : d + 1], (CAP, 128)
        )

    where = (
        lax.rem(own // 2, 8) * 192 + ((own // 16) * 2 + lax.rem(own, 2)) * CAP + slot
    ).astype(F32)
    spos[...] = jnp.broadcast_to(where, (128, TOK)).T

    c_gm.wait()
    lane_low = iota((256, 128), 1) < 64
    for p in range(PAIRS):
        f = slice(p * 128, (p + 1) * 128)
        m = gm[:, 0, f].astype(F32)
        kbd[p, 0:256, :] = jnp.where(lane_low, m, 0.0).astype(BF)
        kbd[p, 256:512, :] = jnp.where(lane_low, 0.0, m).astype(BF)
        m = gm[:, 1, f].astype(F32)
        vbdt[p, :, 0:256] = jnp.where(lane_low, m, 0.0).T.astype(BF)
        vbdt[p, :, 256:512] = jnp.where(lane_low, 0.0, m).T.astype(BF)
    xtok[...] = jnp.zeros((TOK, ENC), BF)
    c_q.wait()

    pl.semaphore_wait(bar, 38)

    loop(1, 32, lambda k: tcopy(lax.rem(dp + k, 32)).start())
    c_lt = pltpu.make_async_copy(reqs.at[dp], rreqs.at[dp], lsem.at[5])
    c_lt.start()
    z_step(0)
    c_lq = pltpu.make_async_copy(packq, gq.at[xl, c, z], lsem.at[3])
    c_lk = pltpu.make_async_copy(packk, gk.at[xl, c, z], lsem.at[4])
    c_lq.start()
    c_lk.start()
    n_out = rdma(q.at[pl.ds(0, 64)], qnext, ns, nr, prv)
    n_out.start()
    z_step(1)

    c_lt.wait()
    loop(1, 32, lambda k: tcopy_in(lax.rem(dp + k, 32)).wait_recv())
    got = jnp.concatenate([rreqs[d] for d in range(32)], axis=0).astype(F32).T
    for d in range(32):
        icol[d] = jnp.broadcast_to(got[0:CAP, d : d + 1], (CAP, 128)).astype(jnp.int32)
    c_emb.wait()

    def dest(zz, j):
        return (j // 2) * 16 + zz * 2 + j % 2

    def rcopy(d, zz, j):
        return rdma(send.at[zz, j], rows.at[z, xl * 2 + c], rs.at[d], rr.at[dp], (seq, d))

    def rcopy_in(d, zz, j):
        return rdma(send.at[zz, j], rows.at[zz, j], rs.at[d], rr.at[d], (seq, d))

    def gather(u):
        for half in range(2):
            zz = lax.rem(z + offset_of(2 * u + half), 8)
            for j in range(4):
                idx = icol[dest(zz, j)]
                base = half * 192 + j * CAP
                for k in range(16):
                    onehot[base : base + CAP, k * 128 : (k + 1) * 128] = (
                        (iota((CAP, 128), 1) + k * 128) == idx
                    ).astype(BF)
        got_rows = nn(onehot[...], emb[...]).astype(BF)
        for half in range(2):
            zz = lax.rem(z + offset_of(2 * u + half), 8)
            for j in range(4):
                base = half * 192 + j * CAP
                send[zz, j] = got_rows[base : base + CAP]

    def row_send(u):
        for half in range(2):
            zz = lax.rem(z + offset_of(2 * u + half), 8)
            for j in range(4):
                d = dest(zz, j)

                @pl.when(d != dp)
                def _():
                    rcopy(d, zz, j).start()

                @pl.when(d == dp)
                def _():
                    pltpu.make_async_copy(send.at[zz, j], rows.at[zz, j], lsem.at[6]).start()

    z_step(2)
    loop(0, 1, gather)
    z_step(3)
    loop(1, 2, gather)
    z_step(4)
    c_lq.wait()
    c_lk.wait()
    y_send(KQ)
    y_send(KK)
    loop(0, 2, row_send)

    def gather_send(u):
        gather(u)
        row_send(u)

    loop(2, 4, gather_send)

    n_out.wait()
    first = iota((64, QW), 0) < 63
    head_rows = jnp.where(first, qnext[...].astype(F32), q[0:64, :].astype(F32)).astype(BF)
    down = (iota((256, 256), 1) == lax.rem(iota((256, 256), 0) + 255, 256)).astype(BF)
    qs[...] = nn(down, jnp.concatenate([head_rows, q[64:256, :]], axis=0)).astype(BF)

    x_send(KQ, 0, 8)
    x_send(KK, 0, 8)
    x_pass(KQ, 0, 8)
    s_wait(KQ)

    f = iota((448, 512), 0)
    perm = (iota((448, 512), 1) == f + 4 * lax.shift_right_logical(f * 2341, 16)).astype(BF)
    for which, dst in ((0, wqt), (2, wot)):
        for a in range(2):
            for d in range(16):
                pieces[d * 32 : (d + 1) * 32, :] = gq[a, d % 2, d // 2, which : which + 2].reshape(32, ENC)
            dst[a * 448 : (a + 1) * 448, :] = nn(perm, pieces[...]).astype(BF)

    def encode(u):
        for half in range(2):
            zz = lax.rem(z + offset_of(2 * u + half), 8)
            for j in range(4):
                d = dest(zz, j)

                @pl.when(d != dp)
                def _():
                    rcopy_in(d, zz, j).wait_recv()

                @pl.when(d == dp)
                def _():
                    pltpu.make_async_copy(send.at[zz, j], rows.at[zz, j], lsem.at[6]).wait()

        zs = [lax.rem(z + offset_of(2 * u + half), 8) for half in range(2)]
        wide = jnp.concatenate([rows[zz].reshape(192, ENC) for zz in zs], axis=0).astype(F32)
        gt = jnp.concatenate([gcol[zz] for zz in zs], axis=0).T[0:8]
        bias = [
            jnp.broadcast_to(jnp.where(gt[0:1] == float(m + 1), 0.0, NEG), (64, UROWS))
            for m in range(4)
        ]
        bias = jnp.concatenate(bias * 2, axis=0)
        inv = lax.rsqrt(jnp.mean(wide * wide, axis=-1, keepdims=True) + 1e-6)
        qenc[...] = nt((wide * inv).astype(BF), wqt[...]).astype(BF)
        for lo, hi in ((0, 4), (4, 7)):
            scores = [nt(kbd[p], qenc[:, p * 128 : (p + 1) * 128]) for p in range(lo, hi)]
            weights = []
            for s in scores:
                s = s * (0.125 * LOG2E) + bias
                for half in range(2):
                    sh = s[half * 256 : (half + 1) * 256]
                    e = jnp.exp2(sh - jnp.max(sh, axis=0, keepdims=True))
                    weights.append((e * (1.0 / jnp.sum(e, axis=0, keepdims=True))).astype(BF))
            for p in range(lo, hi):
                w = jnp.concatenate(weights[2 * (p - lo) : 2 * (p - lo) + 2], axis=0)
                mixed[:, p * 128 : (p + 1) * 128] = nn(vbdt[p], w).T.astype(BF)
        done = (wide + nt(mixed[...], wot[...])).astype(BF)
        lane = iota((1, UROWS), 1)
        want = jnp.where(lane < 192, zs[0] * 192 + lane, zs[1] * 192 + lane - 192).astype(F32)
        move = (jnp.concatenate([spos[...]] * 3, axis=1) == want).astype(BF)
        xtok[...] = xtok[...] + nn(move, done).astype(BF)

    def project(lo, hi):
        for dst, a in ((keys, 0), (vals, 1)):
            for i in range(2):
                w = gk[a, i].reshape(1024, ENC)
                dst[lo:hi, i * 1024 : (i + 1) * 1024] = nt(xtok[lo:hi, :], w).astype(BF)

    def feature(h):
        return ((h % 2) * 8 + h // 2) * HD

    def attend(b, at):
        r = pl.ds(pl.multiple_of(b * 64, 64), 64)
        kr = pl.ds(pl.multiple_of(lax.rem(b + 3, 4) * 256, 256), 256)
        s = [
            nt(qs[r, h * HD : (h + 1) * HD], keys[kr, feature(h) : feature(h) + HD])
            for h in range(HQ)
        ]
        s = jnp.concatenate(s, axis=0) * (LOG2E / math.sqrt(HD))
        e = jnp.exp2(s - jnp.max(s, axis=-1, keepdims=True))
        w = (e * (1.0 / jnp.sum(e, axis=-1, keepdims=True))).astype(BF)
        for h in range(HQ):
            v = vals[kr, feature(h) : feature(h) + HD]
            at[r, h * HD : (h + 1) * HD] = nn(w[h * 64 : (h + 1) * 64], v).astype(BF)

    loop(0, 3, encode)
    x_pass(KK, 0, 8)
    loop(3, 4, encode)
    s_wait(KK)

    project(768, 1024)
    attend(0, out_ref)
    f_out = rdma(out_ref.at[pl.ds(0, 64)], fin, fs, fr, nxt)
    f_out.start()
    project(0, 768)
    loop(1, 4, lambda b: attend(b, out_ref))

    drain(KQ)
    drain(KK)
    loop(1, 32, lambda k: tcopy(lax.rem(dp + k, 32)).wait_send())

    def rdone(i):
        zz = i // 4
        j = lax.rem(i, 4)
        d = (j // 2) * 16 + zz * 2 + lax.rem(j, 2)

        @pl.when(d != dp)
        def _():
            rcopy(d, zz, j).wait_send()

    loop(0, 32, rdone)

    for n, kind, way, count in ZSTEPS:
        for step in range(count):
            zcopy(kind, way, step).wait_send()
    f_out.wait()
    came = jnp.where(seq > 0, 1.0, 0.0).astype(F32) * fin[...].astype(F32)
    mine = out_ref[0:64, :].astype(F32)
    out_ref[0:64, :] = jnp.where(iota((64, QW), 0) < 1, mine, came).astype(BF)


def row_up(in_ref, out_ref):
    up = (iota((256, 256), 1) == lax.rem(iota((256, 256), 0) + 1, 256)).astype(BF)
    out_ref[...] = nn(up, in_ref[...]).astype(BF)


def shards(queries, group_memory, nb_shard, nb_row, embed, w_query_enc, w_out_enc, w_kv_cca):
    own = nb_shard.reshape(1, TOK)
    rid = nb_row.reshape(1, TOK)
    D = pltpu.SemaphoreType.DMA
    vm = lambda *s: pltpu.VMEM(s, BF)
    any_ = pl.BlockSpec(memory_space=pl.ANY)
    here = pl.BlockSpec(memory_space=pltpu.VMEM)
    out = pl.pallas_call(
        body,
        out_shape=jax.ShapeDtypeStruct((256, QW), BF),
        in_specs=[here, here, any_, here, here, here, any_, any_],
        out_specs=here,
        scratch_shapes=[
            vm(2048, ENC), vm(256, 2, ENC), vm(256, QW), vm(4, 32, ENC), vm(4, 16, ENC),
            vm(2, 2, 8, 4, 32, ENC), vm(2, 2, 8, 4, 16, ENC),
            vm(8, 4, CAP, ENC), vm(8, 4, CAP, ENC), vm(UROWS, 2048),
            vm(TOK, QW), vm(TOK, QW), vm(ENC, ENC), vm(ENC, ENC), vm(512, ENC),
            vm(PAIRS, 512, 128), vm(PAIRS, 128, 512),
            pltpu.VMEM((32, 1, 128), jnp.int32), pltpu.VMEM((32, 1, 128), jnp.int32),
            pltpu.VMEM((32, CAP, 128), jnp.int32),
            pltpu.VMEM((8, 192, 128), F32), pltpu.VMEM((TOK, 128), F32),
            vm(TOK, ENC), vm(UROWS, ENC), vm(UROWS, ENC),
            vm(64, QW), vm(256, QW), vm(64, QW),
            D((7,)), D((8,)), D((8,)), D((8,)), D((8,)),
            D((8, 4)), D((8, 4)), D((8, 4)), D((8, 4)),
            D((8,)), D((8,)), D((8,)), D((8,)),
            D((2, 8)), D((2, 8)), D((2, 8)), D((2, 8)),
            D((32,)), D((32,)), D((32,)), D((32,)),
            D(()), D(()), D(()), D(()),
        ],
        compiler_params=pltpu.CompilerParams(
            collective_id=1, has_side_effects=True, vmem_limit_bytes=62 << 20
        ),
    )(own, rid, embed, w_query_enc.T, w_out_enc.T, w_kv_cca, group_memory[0], queries[0])
    block = pl.BlockSpec((256, 512), lambda i: (0, i))
    out = pl.pallas_call(
        row_up,
        grid=(4,),
        out_shape=jax.ShapeDtypeStruct((256, QW), BF),
        in_specs=[block],
        out_specs=block,
    )(out)
    return out[None]


def solution(mesh):
    in_specs = (
        P("dp", "seq", None),
        P("dp", "seq", None, None),
        P("dp", "seq", None, None, None),
        P("dp", "seq", None, None),
        P("dp", None),
        P(None, "dp"),
        P(None, "dp"),
        P(None, "dp"),
    )
    out_specs = P("dp", "seq", None)
    return jax.shard_map(shards, mesh=mesh, in_specs=in_specs, out_specs=out_specs, check_vma=False)
```

```python
import functools
import math

import jax
import jax.numpy as jnp
from jax import lax
from jax.experimental import pallas as pl
from jax.experimental.pallas import tpu as pltpu
from jax.sharding import PartitionSpec as P

MESH = pl.DeviceIdType.MESH
BF = jnp.bfloat16
F32 = jnp.float32
ENC = 896
QW = 2048
HQ = 16
HD = 128
CAP = 48
TOK = 1024
PAIRS = 7
UNITS = 4
UROWS = 384
NEG = -1e30
LOG2E = math.log2(math.e)


def nt(a, b):
    return lax.dot_general(a, b, (((1,), (1,)), ((), ())), preferred_element_type=F32)


def nn(a, b):
    return jnp.dot(a, b, preferred_element_type=F32)


def iota(shape, dim):
    return lax.broadcasted_iota(jnp.int32, shape, dim)


def offset_of(k):
    base = 4 - (k + 1) // 2
    odd = lax.rem(k, 2)
    return lax.rem(odd * base + (1 - odd) * (8 - base), 8)


def body(
    own_ref, rid_ref, emb_hbm, wq_ref, wo_ref, wkv_ref, gm_hbm, q_hbm,
    out_ref,
    emb, gm, q, packk, packq, gk, gq, send, rows, onehot, keys, vals, wqt, wot, pieces,
    kbd, vbdt, reqs, rreqs, icol, gcol, spos, xtok, qenc, mixed, qnext, qs, fin, outp,
    lsem, zks, zkr, zqs, zqr, yks, ykr, yqs, yqr, xks, xkr, xqs, xqr, sks, skr, sqs, sqr,
    rs, rr, ts, tr, ns, nr, fs, fr,
):
    seq = lax.axis_index("seq")
    dp = lax.axis_index("dp")
    xl = dp // 16
    z = lax.rem(dp // 2, 8)
    c = lax.rem(dp, 2)
    y = seq // 2
    xh = lax.rem(seq, 2)
    x = xh * 2 + xl
    xo = 1 - xl

    def at_x(xx):
        return (y * 2 + xx // 2, lax.rem(xx, 2) * 16 + z * 2 + c)

    partner = at_x(x + 1 - 2 * xl)
    wrap = at_x(lax.rem(x + 3 + 2 * xl, 4))
    sib = (seq, xl * 16 + z * 2 + 1 - c)
    nxt = (lax.rem(seq + 1, 8), dp)
    prv = (lax.rem(seq + 7, 8), dp)

    c_emb = pltpu.make_async_copy(emb_hbm, emb, lsem.at[0])
    c_q = pltpu.make_async_copy(q_hbm, q, lsem.at[1])
    c_gm = pltpu.make_async_copy(gm_hbm, gm, lsem.at[2])
    c_emb.start()
    c_q.start()
    c_gm.start()

    bar = pltpu.get_barrier_semaphore()

    def greet(k, _):
        pl.semaphore_signal(bar, inc=1, device_id=(seq, lax.rem(dp + k, 32)), device_id_type=MESH)
        return 0

    lax.fori_loop(1, 32, greet, 0)
    for k in range(1, 4):
        pl.semaphore_signal(bar, inc=1, device_id=(lax.rem(y + k, 4) * 2 + xh, dp), device_id_type=MESH)
    for dev in (partner, wrap, nxt, prv):
        pl.semaphore_signal(bar, inc=1, device_id=dev, device_id_type=MESH)

    kvt = wkv_ref[...].T
    packk[...] = kvt.reshape(4, 32, ENC)
    zero4 = jnp.zeros((4, ENC), BF)
    packq[0] = wq_ref[0:16, :]
    packq[1] = jnp.concatenate([wq_ref[16:28, :].astype(F32), zero4.astype(F32)], axis=0).astype(BF)
    packq[2] = wo_ref[0:16, :]
    packq[3] = jnp.concatenate([wo_ref[16:28, :].astype(F32), zero4.astype(F32)], axis=0).astype(BF)

    def rdma(src, dst, s, r, dev):
        return pltpu.make_async_remote_copy(
            src_ref=src, dst_ref=dst, send_sem=s, recv_sem=r, device_id=dev, device_id_type=MESH
        )

    KQ = (packq, gq, zqs, zqr, yqs, yqr, xqs, xqr, sqs, sqr)
    KK = (packk, gk, zks, zkr, yks, ykr, xks, xkr, sks, skr)

    def zcopy(kind, way, step):
        pack, g, s, r = kind[0], kind[1], kind[2], kind[3]
        of = lax.rem(z - way * step + 8, 8)
        to = lax.rem(z + way + 8, 8)
        src = pack.at[y] if step == 0 else g.at[xl, c, of, y]
        mark = step if way == 1 else 4 + step
        return rdma(src, g.at[xl, c, of, y], s.at[mark], r.at[of], (seq, xl * 16 + to * 2 + c))

    def zcopy_in(kind, way, step):
        pack, g, s, r = kind[0], kind[1], kind[2], kind[3]
        of = lax.rem(z - way * (step + 1) + 8, 8)
        frm = lax.rem(z + way + 8, 8)
        p = g.at[xl, c, of, y]
        return rdma(p, p, s.at[of], r.at[of], (seq, xl * 16 + frm * 2 + c))

    ZSTEPS = ((0, KQ, 1, 4), (1, KQ, -1, 3), (2, KK, -1, 4), (3, KK, 1, 3))

    def z_step(step):
        for n, kind, way, count in ZSTEPS:
            if 0 < step <= count:
                zcopy_in(kind, way, step - 1).wait_recv()
            if step < count:
                zcopy(kind, way, step).start()

    def ycopy(kind, zz, yy):
        g, s, r = kind[1], kind[4], kind[5]
        p = g.at[xl, c, zz, y]
        return rdma(p, p, s.at[zz, yy], r.at[zz, y], (yy * 2 + xh, dp))

    def ycopy_in(kind, zz, yy):
        g, s, r = kind[1], kind[4], kind[5]
        p = g.at[xl, c, zz, yy]
        return rdma(p, p, s.at[zz, yy], r.at[zz, yy], (yy * 2 + xh, dp))

    def xcopy(kind, zz, dev):
        g, s, r = kind[1], kind[6], kind[7]
        p = g.at[xl, c, zz]
        return rdma(p, p, s.at[zz], r.at[zz], dev)

    def xcopy_in(kind, zz):
        g, s, r = kind[1], kind[6], kind[7]
        p = g.at[xo, c, zz]
        return rdma(p, p, s.at[zz], r.at[zz], partner)

    def scopy(kind, a, zz):
        g, s, r = kind[1], kind[8], kind[9]
        p = g.at[a, c, zz]
        return rdma(p, p, s.at[a, zz], r.at[a, zz], sib)

    def scopy_in(kind, a, zz):
        g, s, r = kind[1], kind[8], kind[9]
        p = g.at[a, 1 - c, zz]
        return rdma(p, p, s.at[a, zz], r.at[a, zz], sib)

    def loop(lo, hi, fn):
        def step(k, _):
            fn(k)
            return 0

        lax.fori_loop(lo, hi, step, 0)

    def y_send(kind, lo, hi):
        def one(k):
            zz = lax.rem(z + k, 8)
            for j in range(1, 4):
                ycopy(kind, zz, lax.rem(y + j, 4)).start()

        loop(lo, hi, one)

    def x_send(kind, lo, hi):
        def one(k):
            zz = lax.rem(z + k, 8)

            @pl.when(k > 0)
            def _():
                for j in range(1, 4):
                    ycopy_in(kind, zz, lax.rem(y + j, 4)).wait_recv()

            @pl.when(lax.rem(zz, 3) == 0)
            def _():
                xcopy(kind, zz, partner).start()

            @pl.when(lax.rem(zz, 3) != 0)
            def _():
                xcopy(kind, zz, wrap).start()

            scopy(kind, xl, zz).start()

        loop(lo, hi, one)

    def x_pass(kind, lo, hi):
        def one(k):
            zz = lax.rem(z + k, 8)
            xcopy_in(kind, zz).wait_recv()
            scopy(kind, xo, zz).start()

        loop(lo, hi, one)

    def s_wait(kind):
        def one(zz):
            for a in range(2):
                scopy_in(kind, a, zz).wait_recv()

        loop(0, 8, one)

    def drain_x(kind):
        def one(zz):
            xcopy(kind, zz, partner).wait_send()
            for a in range(2):
                scopy(kind, a, zz).wait_send()

        loop(0, 8, one)

    def drain_y(kind):
        def one(k):
            zz = lax.rem(z + k, 8)
            for j in range(1, 4):
                ycopy(kind, zz, lax.rem(y + j, 4)).wait_send()

        loop(1, 8, one)

    own = own_ref[...]
    marks = (iota((32, TOK), 0) == own).astype(F32)
    upper = (iota((128, 128), 0) <= iota((128, 128), 1)).astype(BF)
    total = jnp.zeros((32, 1), F32)
    parts = []
    for k in range(TOK // 128):
        m = marks[:, k * 128 : (k + 1) * 128]
        cum = nn(m.astype(BF), upper) + total
        total = cum[:, 127:128]
        parts.append(jnp.sum(m * (cum - 1.0), axis=0, keepdims=True))
    slot = jnp.concatenate(parts, axis=1).astype(jnp.int32)
    place = (iota((128, TOK), 0) == slot).astype(BF)
    rid = rid_ref[...]
    high = (rid // 64).astype(F32)
    low = (rid - (rid // 64) * 64).astype(F32)
    group = (iota((1, TOK), 1) // 256 + 1).astype(F32)
    hi = nt((marks * high).astype(BF), place)
    lo = nt((marks * low).astype(BF), place)
    asked = (hi * 64.0 + lo).astype(jnp.int32)
    for d in range(32):
        reqs[d] = asked[d : d + 1, :]

    def tcopy(d):
        return rdma(reqs.at[d], rreqs.at[dp], ts.at[d], tr.at[dp], (seq, d))

    def tcopy_in(d):
        return rdma(reqs.at[d], rreqs.at[d], ts.at[d], tr.at[d], (seq, d))

    groups = nt(place, (marks * group).astype(BF))
    for d in range(32):
        place_d = ((d // 2) % 8) * 4 + (d // 16) * 2 + d % 2
        gcol[place_d // 4, (place_d % 4) * CAP : (place_d % 4 + 1) * CAP, :] = jnp.broadcast_to(
            groups[0:CAP, d : d + 1], (CAP, 128)
        )

    where = (
        lax.rem(own // 2, 8) * 192 + ((own // 16) * 2 + lax.rem(own, 2)) * CAP + slot
    ).astype(F32)
    spos[...] = jnp.broadcast_to(where, (128, TOK)).T

    c_gm.wait()
    lane_low = iota((256, 128), 1) < 64
    for p in range(PAIRS):
        f = slice(p * 128, (p + 1) * 128)
        m = gm[:, 0, f].astype(F32)
        kbd[p, 0:256, :] = jnp.where(lane_low, m, 0.0).astype(BF)
        kbd[p, 256:512, :] = jnp.where(lane_low, 0.0, m).astype(BF)
        m = gm[:, 1, f].astype(F32)
        vbdt[p, :, 0:256] = jnp.where(lane_low, m, 0.0).T.astype(BF)
        vbdt[p, :, 256:512] = jnp.where(lane_low, 0.0, m).T.astype(BF)
    xtok[...] = jnp.zeros((TOK, ENC), BF)
    c_q.wait()

    pl.semaphore_wait(bar, 38)

    loop(1, 32, lambda k: tcopy(lax.rem(dp + k, 32)).start())
    c_lt = pltpu.make_async_copy(reqs.at[dp], rreqs.at[dp], lsem.at[5])
    c_lt.start()
    z_step(0)
    c_lq = pltpu.make_async_copy(packq, gq.at[xl, c, z], lsem.at[3])
    c_lk = pltpu.make_async_copy(packk, gk.at[xl, c, z], lsem.at[4])
    c_lq.start()
    c_lk.start()
    n_out = rdma(q.at[pl.ds(0, 64)], qnext, ns, nr, prv)
    n_out.start()
    z_step(1)

    c_lt.wait()
    loop(1, 32, lambda k: tcopy_in(lax.rem(dp + k, 32)).wait_recv())
    got = jnp.concatenate([rreqs[d] for d in range(32)], axis=0).astype(F32).T
    for d in range(32):
        icol[d] = jnp.broadcast_to(got[0:CAP, d : d + 1], (CAP, 128)).astype(jnp.int32)
    c_emb.wait()

    def dest(zz, j):
        return (j // 2) * 16 + zz * 2 + j % 2

    def rcopy(d, zz, j):
        return rdma(send.at[zz, j], rows.at[z, xl * 2 + c], rs.at[d], rr.at[dp], (seq, d))

    def rcopy_in(d, zz, j):
        return rdma(send.at[zz, j], rows.at[zz, j], rs.at[d], rr.at[d], (seq, d))

    def gather(u):
        for half in range(2):
            zz = lax.rem(z + offset_of(2 * u + half), 8)
            for j in range(4):
                idx = icol[dest(zz, j)]
                base = half * 192 + j * CAP
                for k in range(16):
                    onehot[base : base + CAP, k * 128 : (k + 1) * 128] = (
                        (iota((CAP, 128), 1) + k * 128) == idx
                    ).astype(BF)
        got_rows = nn(onehot[...], emb[...]).astype(BF)
        for half in range(2):
            zz = lax.rem(z + offset_of(2 * u + half), 8)
            for j in range(4):
                base = half * 192 + j * CAP
                send[zz, j] = got_rows[base : base + CAP]

    def row_send(u):
        for half in range(2):
            zz = lax.rem(z + offset_of(2 * u + half), 8)
            for j in range(4):
                d = dest(zz, j)

                @pl.when(d != dp)
                def _():
                    rcopy(d, zz, j).start()

                @pl.when(d == dp)
                def _():
                    pltpu.make_async_copy(send.at[zz, j], rows.at[zz, j], lsem.at[6]).start()

    z_step(2)
    loop(0, 1, gather)
    z_step(3)
    loop(1, 2, gather)
    z_step(4)
    c_lq.wait()
    c_lk.wait()
    y_send(KQ, 1, 8)
    loop(0, 2, row_send)

    def gather_send(u):
        gather(u)
        row_send(u)

    loop(2, 4, gather_send)
    y_send(KK, 1, 5)

    n_out.wait()
    first = iota((64, QW), 0) < 63
    head_rows = jnp.where(first, qnext[...].astype(F32), q[0:64, :].astype(F32)).astype(BF)
    down = (iota((256, 256), 1) == lax.rem(iota((256, 256), 0) + 255, 256)).astype(BF)
    qs[...] = nn(down, jnp.concatenate([head_rows, q[64:256, :]], axis=0)).astype(BF)

    x_send(KQ, 0, 8)
    y_send(KK, 5, 8)
    x_send(KK, 0, 5)
    x_pass(KQ, 0, 8)
    x_send(KK, 5, 8)
    s_wait(KQ)

    f = iota((448, 512), 0)
    perm = (iota((448, 512), 1) == f + 4 * lax.shift_right_logical(f * 2341, 16)).astype(BF)
    for which, dst in ((0, wqt), (2, wot)):
        for a in range(2):
            for d in range(16):
                pieces[d * 32 : (d + 1) * 32, :] = gq[a, d % 2, d // 2, which : which + 2].reshape(32, ENC)
            dst[a * 448 : (a + 1) * 448, :] = nn(perm, pieces[...]).astype(BF)

    def encode(u):
        for half in range(2):
            zz = lax.rem(z + offset_of(2 * u + half), 8)
            for j in range(4):
                d = dest(zz, j)

                @pl.when(d != dp)
                def _():
                    rcopy_in(d, zz, j).wait_recv()

                @pl.when(d == dp)
                def _():
                    pltpu.make_async_copy(send.at[zz, j], rows.at[zz, j], lsem.at[6]).wait()

        zs = [lax.rem(z + offset_of(2 * u + half), 8) for half in range(2)]
        wide = jnp.concatenate([rows[zz].reshape(192, ENC) for zz in zs], axis=0).astype(F32)
        gt = jnp.concatenate([gcol[zz] for zz in zs], axis=0).T[0:8]
        bias = [
            jnp.broadcast_to(jnp.where(gt[0:1] == float(m + 1), 0.0, NEG), (64, UROWS))
            for m in range(4)
        ]
        bias = jnp.concatenate(bias * 2, axis=0)
        inv = lax.rsqrt(jnp.mean(wide * wide, axis=-1, keepdims=True) + 1e-6)
        qenc[...] = nt((wide * inv).astype(BF), wqt[...]).astype(BF)
        for lo, hi in ((0, 4), (4, 7)):
            scores = [nt(kbd[p], qenc[:, p * 128 : (p + 1) * 128]) for p in range(lo, hi)]
            weights = []
            for s in scores:
                s = s * (0.125 * LOG2E) + bias
                for half in range(2):
                    sh = s[half * 256 : (half + 1) * 256]
                    e = jnp.exp2(sh - jnp.max(sh, axis=0, keepdims=True))
                    weights.append((e * (1.0 / jnp.sum(e, axis=0, keepdims=True))).astype(BF))
            for p in range(lo, hi):
                w = jnp.concatenate(weights[2 * (p - lo) : 2 * (p - lo) + 2], axis=0)
                mixed[:, p * 128 : (p + 1) * 128] = nn(vbdt[p], w).T.astype(BF)
        done = (wide + nt(mixed[...], wot[...])).astype(BF)
        lane = iota((1, UROWS), 1)
        want = jnp.where(lane < 192, zs[0] * 192 + lane, zs[1] * 192 + lane - 192).astype(F32)
        move = (jnp.concatenate([spos[...]] * 3, axis=1) == want).astype(BF)
        xtok[...] = xtok[...] + nn(move, done).astype(BF)

    def project(lo, hi):
        for dst, a in ((keys, 0), (vals, 1)):
            for i in range(2):
                w = gk[a, i].reshape(1024, ENC)
                dst[lo:hi, i * 1024 : (i + 1) * 1024] = nt(xtok[lo:hi, :], w).astype(BF)

    def feature(h):
        return ((h % 2) * 8 + h // 2) * HD

    def attend(b, at):
        r = pl.ds(pl.multiple_of(b * 64, 64), 64)
        kr = pl.ds(pl.multiple_of(lax.rem(b + 3, 4) * 256, 256), 256)
        s = [
            nt(qs[r, h * HD : (h + 1) * HD], keys[kr, feature(h) : feature(h) + HD])
            for h in range(HQ)
        ]
        s = jnp.concatenate(s, axis=0) * (LOG2E / math.sqrt(HD))
        e = jnp.exp2(s - jnp.max(s, axis=-1, keepdims=True))
        w = (e * (1.0 / jnp.sum(e, axis=-1, keepdims=True))).astype(BF)
        for h in range(HQ):
            v = vals[kr, feature(h) : feature(h) + HD]
            at[r, h * HD : (h + 1) * HD] = nn(w[h * 64 : (h + 1) * 64], v).astype(BF)

    loop(0, 3, encode)
    x_pass(KK, 0, 8)
    drain_y(KQ)
    drain_y(KK)
    drain_x(KQ)
    loop(1, 32, lambda k: tcopy(lax.rem(dp + k, 32)).wait_send())
    for n, kind, way, count in ZSTEPS:
        for step in range(count):
            zcopy(kind, way, step).wait_send()
    loop(3, 4, encode)
    s_wait(KK)

    project(768, 1024)
    attend(0, outp)
    f_out = rdma(outp.at[pl.ds(0, 64)], fin, fs, fr, nxt)
    f_out.start()
    project(0, 768)
    loop(1, 4, lambda b: attend(b, outp))

    drain_x(KK)

    def rdone(i):
        zz = i // 4
        j = lax.rem(i, 4)
        d = (j // 2) * 16 + zz * 2 + lax.rem(j, 2)

        @pl.when(d != dp)
        def _():
            rcopy(d, zz, j).wait_send()

    loop(0, 32, rdone)

    f_out.wait()
    came = jnp.where(seq > 0, 1.0, 0.0).astype(F32) * fin[...].astype(F32)
    mine = outp[0:64, :].astype(F32)
    top = jnp.where(iota((64, QW), 0) < 1, mine, came).astype(BF)
    up = (iota((256, 256), 1) == lax.rem(iota((256, 256), 0) + 1, 256)).astype(BF)
    out_ref[...] = nn(up, jnp.concatenate([top, outp[64:256, :]], axis=0)).astype(BF)


def shards(queries, group_memory, nb_shard, nb_row, embed, w_query_enc, w_out_enc, w_kv_cca):
    own = nb_shard.reshape(1, TOK)
    rid = nb_row.reshape(1, TOK)
    D = pltpu.SemaphoreType.DMA
    vm = lambda *s: pltpu.VMEM(s, BF)
    any_ = pl.BlockSpec(memory_space=pl.ANY)
    here = pl.BlockSpec(memory_space=pltpu.VMEM)
    out = pl.pallas_call(
        body,
        out_shape=jax.ShapeDtypeStruct((256, QW), BF),
        in_specs=[here, here, any_, here, here, here, any_, any_],
        out_specs=here,
        scratch_shapes=[
            vm(2048, ENC), vm(256, 2, ENC), vm(256, QW), vm(4, 32, ENC), vm(4, 16, ENC),
            vm(2, 2, 8, 4, 32, ENC), vm(2, 2, 8, 4, 16, ENC),
            vm(8, 4, CAP, ENC), vm(8, 4, CAP, ENC), vm(UROWS, 2048),
            vm(TOK, QW), vm(TOK, QW), vm(ENC, ENC), vm(ENC, ENC), vm(512, ENC),
            vm(PAIRS, 512, 128), vm(PAIRS, 128, 512),
            pltpu.VMEM((32, 1, 128), jnp.int32), pltpu.VMEM((32, 1, 128), jnp.int32),
            pltpu.VMEM((32, CAP, 128), jnp.int32),
            pltpu.VMEM((8, 192, 128), F32), pltpu.VMEM((TOK, 128), F32),
            vm(TOK, ENC), vm(UROWS, ENC), vm(UROWS, ENC),
            vm(64, QW), vm(256, QW), vm(64, QW), vm(256, QW),
            D((7,)), D((8,)), D((8,)), D((8,)), D((8,)),
            D((8, 4)), D((8, 4)), D((8, 4)), D((8, 4)),
            D((8,)), D((8,)), D((8,)), D((8,)),
            D((2, 8)), D((2, 8)), D((2, 8)), D((2, 8)),
            D((32,)), D((32,)), D((32,)), D((32,)),
            D(()), D(()), D(()), D(()),
        ],
        compiler_params=pltpu.CompilerParams(
            collective_id=1, has_side_effects=True, vmem_limit_bytes=62 << 20
        ),
    )(own, rid, embed, w_query_enc.T, w_out_enc.T, w_kv_cca, group_memory[0], queries[0])
    return out[None]


def solution(mesh):
    in_specs = (
        P("dp", "seq", None),
        P("dp", "seq", None, None),
        P("dp", "seq", None, None, None),
        P("dp", "seq", None, None),
        P("dp", None),
        P(None, "dp"),
        P(None, "dp"),
        P(None, "dp"),
    )
    out_specs = P("dp", "seq", None)
    return jax.shard_map(shards, mesh=mesh, in_specs=in_specs, out_specs=out_specs, check_vma=False)
```

```python
import functools
import math

import jax
import jax.numpy as jnp
from jax import lax
from jax.experimental import pallas as pl
from jax.experimental.pallas import tpu as pltpu
from jax.sharding import PartitionSpec as P

MESH = pl.DeviceIdType.MESH
BF = jnp.bfloat16
F32 = jnp.float32
ENC = 896
QW = 2048
HQ = 16
HD = 128
CAP = 48
TOK = 1024
PAIRS = 7
UNITS = 4
UROWS = 384
NEG = -1e30
LOG2E = math.log2(math.e)


def nt(a, b):
    return lax.dot_general(a, b, (((1,), (1,)), ((), ())), preferred_element_type=F32)


def nn(a, b):
    return jnp.dot(a, b, preferred_element_type=F32)


def iota(shape, dim):
    return lax.broadcasted_iota(jnp.int32, shape, dim)


def offset_of(k):
    a = lax.rem(k // 2, 2)
    b = k // 4
    odd = lax.rem(k, 2)
    base = 3 + a - b - 2 * a * b
    return (1 - odd) * base + odd * lax.rem(8 - base - 4 * a * (1 - b), 8)


def body(
    own_ref, rid_ref, emb_hbm, wq_ref, wo_ref, wkv_ref, gm_hbm, q_hbm,
    out_ref,
    emb, gm, q, packk, packq, gk, gq, send, rows, onehot, keys, vals, wqt, wot, pieces,
    kbd, vbdt, reqs, rreqs, icol, gcol, spos, xtok, qenc, mixed, qnext, qs, fin, outp,
    lsem, zks, zkr, zqs, zqr, yks, ykr, yqs, yqr, xks, xkr, xqs, xqr, sks, skr, sqs, sqr,
    rs, rr, ts, tr, ns, nr, fs, fr,
):
    seq = lax.axis_index("seq")
    dp = lax.axis_index("dp")
    xl = dp // 16
    z = lax.rem(dp // 2, 8)
    c = lax.rem(dp, 2)
    y = seq // 2
    xh = lax.rem(seq, 2)
    x = xh * 2 + xl
    xo = 1 - xl

    def at_x(xx):
        return (y * 2 + xx // 2, lax.rem(xx, 2) * 16 + z * 2 + c)

    partner = at_x(x + 1 - 2 * xl)
    wrap = at_x(lax.rem(x + 3 + 2 * xl, 4))
    sib = (seq, xl * 16 + z * 2 + 1 - c)
    nxt = (lax.rem(seq + 1, 8), dp)
    prv = (lax.rem(seq + 7, 8), dp)

    c_emb = pltpu.make_async_copy(emb_hbm, emb, lsem.at[0])
    c_q = pltpu.make_async_copy(q_hbm, q, lsem.at[1])
    c_gm = pltpu.make_async_copy(gm_hbm, gm, lsem.at[2])
    c_emb.start()
    c_q.start()
    c_gm.start()

    bar = pltpu.get_barrier_semaphore()

    def greet(k, _):
        pl.semaphore_signal(bar, inc=1, device_id=(seq, lax.rem(dp + k, 32)), device_id_type=MESH)
        return 0

    lax.fori_loop(1, 32, greet, 0)
    for k in range(1, 4):
        pl.semaphore_signal(bar, inc=1, device_id=(lax.rem(y + k, 4) * 2 + xh, dp), device_id_type=MESH)
    for dev in (partner, wrap, nxt, prv):
        pl.semaphore_signal(bar, inc=1, device_id=dev, device_id_type=MESH)

    kvt = wkv_ref[...].T
    packk[...] = kvt.reshape(4, 32, ENC)
    zero4 = jnp.zeros((4, ENC), BF)
    packq[0] = wq_ref[0:16, :]
    packq[1] = jnp.concatenate([wq_ref[16:28, :].astype(F32), zero4.astype(F32)], axis=0).astype(BF)
    packq[2] = wo_ref[0:16, :]
    packq[3] = jnp.concatenate([wo_ref[16:28, :].astype(F32), zero4.astype(F32)], axis=0).astype(BF)

    def rdma(src, dst, s, r, dev):
        return pltpu.make_async_remote_copy(
            src_ref=src, dst_ref=dst, send_sem=s, recv_sem=r, device_id=dev, device_id_type=MESH
        )

    KQ = (packq, gq, zqs, zqr, yqs, yqr, xqs, xqr, sqs, sqr)
    KK = (packk, gk, zks, zkr, yks, ykr, xks, xkr, sks, skr)

    def zcopy(kind, way, step):
        pack, g, s, r = kind[0], kind[1], kind[2], kind[3]
        of = lax.rem(z - way * step + 8, 8)
        to = lax.rem(z + way + 8, 8)
        src = pack.at[y] if step == 0 else g.at[xl, c, of, y]
        mark = step if way == 1 else 4 + step
        return rdma(src, g.at[xl, c, of, y], s.at[mark], r.at[of], (seq, xl * 16 + to * 2 + c))

    def zcopy_in(kind, way, step):
        pack, g, s, r = kind[0], kind[1], kind[2], kind[3]
        of = lax.rem(z - way * (step + 1) + 8, 8)
        frm = lax.rem(z + way + 8, 8)
        p = g.at[xl, c, of, y]
        return rdma(p, p, s.at[of], r.at[of], (seq, xl * 16 + frm * 2 + c))

    ZSTEPS = ((0, KQ, 1, 4), (1, KQ, -1, 3), (2, KK, -1, 4), (3, KK, 1, 3))

    def z_step(step):
        for n, kind, way, count in ZSTEPS:
            if 0 < step <= count:
                zcopy_in(kind, way, step - 1).wait_recv()
            if step < count:
                zcopy(kind, way, step).start()

    def ycopy(kind, zz, yy):
        g, s, r = kind[1], kind[4], kind[5]
        p = g.at[xl, c, zz, y]
        return rdma(p, p, s.at[zz, yy], r.at[zz, y], (yy * 2 + xh, dp))

    def ycopy_in(kind, zz, yy):
        g, s, r = kind[1], kind[4], kind[5]
        p = g.at[xl, c, zz, yy]
        return rdma(p, p, s.at[zz, yy], r.at[zz, yy], (yy * 2 + xh, dp))

    def xcopy(kind, zz, dev):
        g, s, r = kind[1], kind[6], kind[7]
        p = g.at[xl, c, zz]
        return rdma(p, p, s.at[zz], r.at[zz], dev)

    def xcopy_in(kind, zz):
        g, s, r = kind[1], kind[6], kind[7]
        p = g.at[xo, c, zz]
        return rdma(p, p, s.at[zz], r.at[zz], partner)

    def scopy(kind, a, zz):
        g, s, r = kind[1], kind[8], kind[9]
        p = g.at[a, c, zz]
        return rdma(p, p, s.at[a, zz], r.at[a, zz], sib)

    def scopy_in(kind, a, zz):
        g, s, r = kind[1], kind[8], kind[9]
        p = g.at[a, 1 - c, zz]
        return rdma(p, p, s.at[a, zz], r.at[a, zz], sib)

    def loop(lo, hi, fn):
        def step(k, _):
            fn(k)
            return 0

        lax.fori_loop(lo, hi, step, 0)

    def y_send(kind, lo, hi):
        def one(k):
            zz = lax.rem(z + k, 8)
            for j in range(1, 4):
                ycopy(kind, zz, lax.rem(y + j, 4)).start()

        loop(lo, hi, one)

    def x_send(kind, lo, hi):
        def one(k):
            zz = lax.rem(z + k, 8)

            @pl.when(k > 0)
            def _():
                for j in range(1, 4):
                    ycopy_in(kind, zz, lax.rem(y + j, 4)).wait_recv()

            @pl.when(lax.rem(zz, 3) == 0)
            def _():
                xcopy(kind, zz, partner).start()

            @pl.when(lax.rem(zz, 3) != 0)
            def _():
                xcopy(kind, zz, wrap).start()

            scopy(kind, xl, zz).start()

        loop(lo, hi, one)

    def x_pass(kind, lo, hi):
        def one(k):
            zz = lax.rem(z + k, 8)
            xcopy_in(kind, zz).wait_recv()
            scopy(kind, xo, zz).start()

        loop(lo, hi, one)

    def s_wait(kind):
        def one(zz):
            for a in range(2):
                scopy_in(kind, a, zz).wait_recv()

        loop(0, 8, one)

    def drain_x(kind):
        def one(zz):
            xcopy(kind, zz, partner).wait_send()
            for a in range(2):
                scopy(kind, a, zz).wait_send()

        loop(0, 8, one)

    def drain_y(kind):
        def one(k):
            zz = lax.rem(z + k, 8)
            for j in range(1, 4):
                ycopy(kind, zz, lax.rem(y + j, 4)).wait_send()

        loop(1, 8, one)

    own = own_ref[...]
    marks = (iota((32, TOK), 0) == own).astype(F32)
    upper = (iota((128, 128), 0) <= iota((128, 128), 1)).astype(BF)
    total = jnp.zeros((32, 1), F32)
    parts = []
    for k in range(TOK // 128):
        m = marks[:, k * 128 : (k + 1) * 128]
        cum = nn(m.astype(BF), upper) + total
        total = cum[:, 127:128]
        parts.append(jnp.sum(m * (cum - 1.0), axis=0, keepdims=True))
    slot = jnp.concatenate(parts, axis=1).astype(jnp.int32)
    place = (iota((128, TOK), 0) == slot).astype(BF)
    rid = rid_ref[...]
    high = (rid // 64).astype(F32)
    low = (rid - (rid // 64) * 64).astype(F32)
    group = (iota((1, TOK), 1) // 256 + 1).astype(F32)
    hi = nt((marks * high).astype(BF), place)
    lo = nt((marks * low).astype(BF), place)
    asked = (hi * 64.0 + lo).astype(jnp.int32)
    for d in range(32):
        reqs[d] = asked[d : d + 1, :]

    def tcopy(d):
        return rdma(reqs.at[d], rreqs.at[dp], ts.at[d], tr.at[dp], (seq, d))

    def tcopy_in(d):
        return rdma(reqs.at[d], rreqs.at[d], ts.at[d], tr.at[d], (seq, d))

    groups = nt(place, (marks * group).astype(BF))
    for d in range(32):
        place_d = ((d // 2) % 8) * 4 + (d // 16) * 2 + d % 2
        gcol[place_d // 4, (place_d % 4) * CAP : (place_d % 4 + 1) * CAP, :] = jnp.broadcast_to(
            groups[0:CAP, d : d + 1], (CAP, 128)
        )

    where = (
        lax.rem(own // 2, 8) * 192 + ((own // 16) * 2 + lax.rem(own, 2)) * CAP + slot
    ).astype(F32)
    spos[...] = jnp.broadcast_to(where, (128, TOK)).T

    c_gm.wait()
    lane_low = iota((256, 128), 1) < 64
    for p in range(PAIRS):
        f = slice(p * 128, (p + 1) * 128)
        m = gm[:, 0, f].astype(F32)
        kbd[p, 0:256, :] = jnp.where(lane_low, m, 0.0).astype(BF)
        kbd[p, 256:512, :] = jnp.where(lane_low, 0.0, m).astype(BF)
        m = gm[:, 1, f].astype(F32)
        vbdt[p, :, 0:256] = jnp.where(lane_low, m, 0.0).T.astype(BF)
        vbdt[p, :, 256:512] = jnp.where(lane_low, 0.0, m).T.astype(BF)
    xtok[...] = jnp.zeros((TOK, ENC), BF)
    c_q.wait()

    pl.semaphore_wait(bar, 38)

    loop(1, 32, lambda k: tcopy(lax.rem(dp + k, 32)).start())
    c_lt = pltpu.make_async_copy(reqs.at[dp], rreqs.at[dp], lsem.at[5])
    c_lt.start()
    z_step(0)
    c_lq = pltpu.make_async_copy(packq, gq.at[xl, c, z], lsem.at[3])
    c_lk = pltpu.make_async_copy(packk, gk.at[xl, c, z], lsem.at[4])
    c_lq.start()
    c_lk.start()
    n_out = rdma(q.at[pl.ds(0, 64)], qnext, ns, nr, prv)
    n_out.start()
    z_step(1)

    c_lt.wait()
    loop(1, 32, lambda k: tcopy_in(lax.rem(dp + k, 32)).wait_recv())
    got = jnp.concatenate([rreqs[d] for d in range(32)], axis=0).astype(F32).T
    for d in range(32):
        icol[d] = jnp.broadcast_to(got[0:CAP, d : d + 1], (CAP, 128)).astype(jnp.int32)
    c_emb.wait()

    def dest(zz, j):
        return (j // 2) * 16 + zz * 2 + j % 2

    def rcopy(d, zz, j):
        return rdma(send.at[zz, j], rows.at[z, xl * 2 + c], rs.at[d], rr.at[dp], (seq, d))

    def rcopy_in(d, zz, j):
        return rdma(send.at[zz, j], rows.at[zz, j], rs.at[d], rr.at[d], (seq, d))

    def gather(u):
        for half in range(2):
            zz = lax.rem(z + offset_of(2 * u + half), 8)
            for j in range(4):
                idx = icol[dest(zz, j)]
                base = half * 192 + j * CAP
                for k in range(16):
                    onehot[base : base + CAP, k * 128 : (k + 1) * 128] = (
                        (iota((CAP, 128), 1) + k * 128) == idx
                    ).astype(BF)
        got_rows = nn(onehot[...], emb[...]).astype(BF)
        for half in range(2):
            zz = lax.rem(z + offset_of(2 * u + half), 8)
            for j in range(4):
                base = half * 192 + j * CAP
                send[zz, j] = got_rows[base : base + CAP]

    def row_send(u):
        for half in range(2):
            zz = lax.rem(z + offset_of(2 * u + half), 8)
            for j in range(4):
                d = dest(zz, j)

                @pl.when(d != dp)
                def _():
                    rcopy(d, zz, j).start()

                @pl.when(d == dp)
                def _():
                    pltpu.make_async_copy(send.at[zz, j], rows.at[zz, j], lsem.at[6]).start()

    z_step(2)
    loop(0, 1, gather)
    z_step(3)
    loop(1, 2, gather)
    z_step(4)
    loop(0, 2, row_send)
    c_lq.wait()
    c_lk.wait()
    y_send(KQ, 1, 8)

    def gather_send(u):
        gather(u)
        row_send(u)

    loop(2, 4, gather_send)
    y_send(KK, 1, 5)

    n_out.wait()
    first = iota((64, QW), 0) < 63
    head_rows = jnp.where(first, qnext[...].astype(F32), q[0:64, :].astype(F32)).astype(BF)
    down = (iota((256, 256), 1) == lax.rem(iota((256, 256), 0) + 255, 256)).astype(BF)
    qs[...] = nn(down, jnp.concatenate([head_rows, q[64:256, :]], axis=0)).astype(BF)

    x_send(KQ, 0, 8)
    y_send(KK, 5, 8)
    x_send(KK, 0, 5)
    x_pass(KQ, 0, 8)
    x_send(KK, 5, 8)
    s_wait(KQ)

    f = iota((448, 512), 0)
    perm = (iota((448, 512), 1) == f + 4 * lax.shift_right_logical(f * 2341, 16)).astype(BF)
    for which, dst in ((0, wqt), (2, wot)):
        for a in range(2):
            for d in range(16):
                pieces[d * 32 : (d + 1) * 32, :] = gq[a, d % 2, d // 2, which : which + 2].reshape(32, ENC)
            dst[a * 448 : (a + 1) * 448, :] = nn(perm, pieces[...]).astype(BF)

    def encode(u):
        for half in range(2):
            zz = lax.rem(z + offset_of(2 * u + half), 8)
            for j in range(4):
                d = dest(zz, j)

                @pl.when(d != dp)
                def _():
                    rcopy_in(d, zz, j).wait_recv()

                @pl.when(d == dp)
                def _():
                    pltpu.make_async_copy(send.at[zz, j], rows.at[zz, j], lsem.at[6]).wait()

        zs = [lax.rem(z + offset_of(2 * u + half), 8) for half in range(2)]
        wide = jnp.concatenate([rows[zz].reshape(192, ENC) for zz in zs], axis=0).astype(F32)
        gt = jnp.concatenate([gcol[zz] for zz in zs], axis=0).T[0:8]
        bias = [
            jnp.broadcast_to(jnp.where(gt[0:1] == float(m + 1), 0.0, NEG), (64, UROWS))
            for m in range(4)
        ]
        bias = jnp.concatenate(bias * 2, axis=0)
        inv = lax.rsqrt(jnp.mean(wide * wide, axis=-1, keepdims=True) + 1e-6)
        qenc[...] = nt((wide * inv).astype(BF), wqt[...]).astype(BF)
        for lo, hi in ((0, 4), (4, 7)):
            scores = [nt(kbd[p], qenc[:, p * 128 : (p + 1) * 128]) for p in range(lo, hi)]
            weights = []
            for s in scores:
                s = s * (0.125 * LOG2E) + bias
                for half in range(2):
                    sh = s[half * 256 : (half + 1) * 256]
                    e = jnp.exp2(sh - jnp.max(sh, axis=0, keepdims=True))
                    weights.append((e * (1.0 / jnp.sum(e, axis=0, keepdims=True))).astype(BF))
            for p in range(lo, hi):
                w = jnp.concatenate(weights[2 * (p - lo) : 2 * (p - lo) + 2], axis=0)
                mixed[:, p * 128 : (p + 1) * 128] = nn(vbdt[p], w).T.astype(BF)
        done = (wide + nt(mixed[...], wot[...])).astype(BF)
        lane = iota((1, UROWS), 1)
        want = jnp.where(lane < 192, zs[0] * 192 + lane, zs[1] * 192 + lane - 192).astype(F32)
        move = (jnp.concatenate([spos[...]] * 3, axis=1) == want).astype(BF)
        xtok[...] = xtok[...] + nn(move, done).astype(BF)

    def project(lo, hi):
        for dst, a in ((keys, 0), (vals, 1)):
            for i in range(2):
                w = gk[a, i].reshape(1024, ENC)
                dst[lo:hi, i * 1024 : (i + 1) * 1024] = nt(xtok[lo:hi, :], w).astype(BF)

    def feature(h):
        return ((h % 2) * 8 + h // 2) * HD

    def attend(b, at):
        r = pl.ds(pl.multiple_of(b * 64, 64), 64)
        kr = pl.ds(pl.multiple_of(lax.rem(b + 3, 4) * 256, 256), 256)
        s = [
            nt(qs[r, h * HD : (h + 1) * HD], keys[kr, feature(h) : feature(h) + HD])
            for h in range(HQ)
        ]
        s = jnp.concatenate(s, axis=0) * (LOG2E / math.sqrt(HD))
        e = jnp.exp2(s - jnp.max(s, axis=-1, keepdims=True))
        w = (e * (1.0 / jnp.sum(e, axis=-1, keepdims=True))).astype(BF)
        for h in range(HQ):
            v = vals[kr, feature(h) : feature(h) + HD]
            at[r, h * HD : (h + 1) * HD] = nn(w[h * 64 : (h + 1) * 64], v).astype(BF)

    loop(0, 3, encode)
    x_pass(KK, 0, 8)
    drain_y(KQ)
    drain_y(KK)
    drain_x(KQ)
    loop(1, 32, lambda k: tcopy(lax.rem(dp + k, 32)).wait_send())
    for n, kind, way, count in ZSTEPS:
        for step in range(count):
            zcopy(kind, way, step).wait_send()
    loop(3, 4, encode)
    s_wait(KK)

    project(768, 1024)
    attend(0, outp)
    f_out = rdma(outp.at[pl.ds(0, 64)], fin, fs, fr, nxt)
    f_out.start()
    project(0, 768)
    loop(1, 4, lambda b: attend(b, outp))

    drain_x(KK)

    def rdone(i):
        zz = i // 4
        j = lax.rem(i, 4)
        d = (j // 2) * 16 + zz * 2 + lax.rem(j, 2)

        @pl.when(d != dp)
        def _():
            rcopy(d, zz, j).wait_send()

    loop(0, 32, rdone)

    f_out.wait()
    came = jnp.where(seq > 0, 1.0, 0.0).astype(F32) * fin[...].astype(F32)
    mine = outp[0:64, :].astype(F32)
    top = jnp.where(iota((64, QW), 0) < 1, mine, came).astype(BF)
    up = (iota((256, 256), 1) == lax.rem(iota((256, 256), 0) + 1, 256)).astype(BF)
    out_ref[...] = nn(up, jnp.concatenate([top, outp[64:256, :]], axis=0)).astype(BF)


def shards(queries, group_memory, nb_shard, nb_row, embed, w_query_enc, w_out_enc, w_kv_cca):
    own = nb_shard.reshape(1, TOK)
    rid = nb_row.reshape(1, TOK)
    D = pltpu.SemaphoreType.DMA
    vm = lambda *s: pltpu.VMEM(s, BF)
    any_ = pl.BlockSpec(memory_space=pl.ANY)
    here = pl.BlockSpec(memory_space=pltpu.VMEM)
    out = pl.pallas_call(
        body,
        out_shape=jax.ShapeDtypeStruct((256, QW), BF),
        in_specs=[here, here, any_, here, here, here, any_, any_],
        out_specs=here,
        scratch_shapes=[
            vm(2048, ENC), vm(256, 2, ENC), vm(256, QW), vm(4, 32, ENC), vm(4, 16, ENC),
            vm(2, 2, 8, 4, 32, ENC), vm(2, 2, 8, 4, 16, ENC),
            vm(8, 4, CAP, ENC), vm(8, 4, CAP, ENC), vm(UROWS, 2048),
            vm(TOK, QW), vm(TOK, QW), vm(ENC, ENC), vm(ENC, ENC), vm(512, ENC),
            vm(PAIRS, 512, 128), vm(PAIRS, 128, 512),
            pltpu.VMEM((32, 1, 128), jnp.int32), pltpu.VMEM((32, 1, 128), jnp.int32),
            pltpu.VMEM((32, CAP, 128), jnp.int32),
            pltpu.VMEM((8, 192, 128), F32), pltpu.VMEM((TOK, 128), F32),
            vm(TOK, ENC), vm(UROWS, ENC), vm(UROWS, ENC),
            vm(64, QW), vm(256, QW), vm(64, QW), vm(256, QW),
            D((7,)), D((8,)), D((8,)), D((8,)), D((8,)),
            D((8, 4)), D((8, 4)), D((8, 4)), D((8, 4)),
            D((8,)), D((8,)), D((8,)), D((8,)),
            D((2, 8)), D((2, 8)), D((2, 8)), D((2, 8)),
            D((32,)), D((32,)), D((32,)), D((32,)),
            D(()), D(()), D(()), D(()),
        ],
        compiler_params=pltpu.CompilerParams(
            collective_id=1, has_side_effects=True, vmem_limit_bytes=62 << 20
        ),
    )(own, rid, embed, w_query_enc.T, w_out_enc.T, w_kv_cca, group_memory[0], queries[0])
    return out[None]


def solution(mesh):
    in_specs = (
        P("dp", "seq", None),
        P("dp", "seq", None, None),
        P("dp", "seq", None, None, None),
        P("dp", "seq", None, None),
        P("dp", None),
        P(None, "dp"),
        P(None, "dp"),
        P(None, "dp"),
    )
    out_specs = P("dp", "seq", None)
    return jax.shard_map(shards, mesh=mesh, in_specs=in_specs, out_specs=out_specs, check_vma=False)
```
